256 devices in a mesh: dp: 16 (over y, x_hi, core), tensor: 16 (over z, x_lo).
Axes of the slice: x: 4 (x_hi: 2, x_lo: 2; x = x_hi * 2 + x_lo), y: 4, z: 8, core: 2. Of those that a mesh axis runs over, the one named last changes fastest.
Arguments:
- activations: bfloat16 [8192, 8192], P('dp'), may hold values from -6 to 6
- basis: bfloat16 [8192, 512], P('dp'), may hold values from -0.25 to 0.25
- out_grads: bfloat16 [8192, 28672], P('dp', 'tensor'), may hold values from -0.046875 to 0.046875
- first_moment: float32 [512, 28672], P('dp', 'tensor'), may hold values from -6 to 6
- second_moment: float32 [512, 28672], P('dp', 'tensor'), may hold values from 0.01 to 0.1
Outputs:
- weight_update: bfloat16 [8192, 28672], P('dp', 'tensor')
- new_first: float32 [512, 28672], P('dp', 'tensor')
- new_second: float32 [512, 28672], P('dp', 'tensor')
The draws below stay inside these ranges and needn't reach their ends.
All inputs are finite; a program needn't handle non-finite values.
Results may differ from the reference program's by a relative error of at most 0.0051.
Values may be sent and summed in bfloat16 or wider, within the bound.
A program may use at most 64 MiB of HBM per device.

```python
import math
import jax
import jax.numpy as jnp

D = 8192
FF = 28672
R = 512
TOKENS = 8192


def level_of(rng, extent, pieces, least, high):
    factor_of, own = 1.0, jax.random.fold_in(rng, 6)
    for axis_at, shards_of in pieces:
        heights = jnp.exp(jax.random.uniform(jax.random.fold_in(own, axis_at), (shards_of,), jnp.float32, least / len(pieces), high / len(pieces)))
        factor_of = factor_of * jnp.repeat(heights, extent[axis_at] // shards_of).reshape([-1 if axis == axis_at else 1 for axis in range(len(extent))])
    return factor_of


def noise(own_key, shape, spread, limit, cuts=(), kind=jnp.bfloat16):
    factor_of = level_of(own_key, shape, cuts, -0.22, 0.18) if cuts else 1.0
    drawn = jax.random.normal(own_key, shape, jnp.float32) * spread * factor_of
    return jnp.minimum(jnp.maximum(drawn, -limit), limit).astype(kind)


def setup_inputs(seed: int = 0) -> dict:
    streams_of = jax.random.split(jax.random.key(seed), 6)
    return {
        "activations": noise(streams_of[0], (TOKENS, D), 1.0, 6.0, ((0, 16),)),
        "basis": noise(streams_of[1], (D, R), R ** -0.5, 0.25, ((0, 16),)),
        "out_grads": noise(streams_of[2], (TOKENS, FF), (0.75 * TOKENS ** -0.5), 0.046875, ((0, 16), (1, 16))),
        "first_moment": noise(streams_of[3], (R, FF), 1.0, 6.0, ((0, 16), (1, 16)), jnp.float32),
        "second_moment": jnp.clip(jnp.exp(math.log(0.1) - 2.3025851 * jax.random.uniform(streams_of[4], (R, FF), jnp.float32) ** level_of(streams_of[4], (R, FF), ((0, 16), (1, 16)), -0.2, 0.2)), 0.01, 0.1),
    }


beta_one = 0.9
beta_two = 0.999
first_fix = 1.0 - 0.9 ** 50
second_fix = 1.0 - 0.999 ** 50
adam_eps = 1e-08

def reference(activations, basis, out_grads, first_moment, second_moment):
    projected = jnp.dot(activations, basis, preferred_element_type=jnp.float32).astype(jnp.bfloat16)
    low_grad = jnp.dot(projected.T, out_grads, preferred_element_type=jnp.float32)
    new_first = beta_one * first_moment + (1.0 - beta_one) * low_grad
    new_second = beta_two * second_moment + (1.0 - beta_two) * low_grad * low_grad
    direction = (new_first / first_fix / (jnp.sqrt(new_second / second_fix) + adam_eps)).astype(jnp.bfloat16)
    weight_update = jnp.dot(basis, direction, preferred_element_type=jnp.float32).astype(jnp.bfloat16)
    return (weight_update, new_first, new_second)
```

```python
import functools

import jax
import jax.numpy as jnp
from jax import lax
from jax.experimental import pallas as pl
from jax.experimental.pallas import tpu as pltpu
from jax.sharding import PartitionSpec as P

beta_one = 0.9
beta_two = 0.999
first_fix = 1.0 - 0.9**50
second_fix = 1.0 - 0.999**50
adam_eps = 1e-08

MESH = pl.DeviceIdType.MESH
bf16 = jnp.bfloat16
f32 = jnp.float32

CHIPS = 8
NEAR = ((1, 0), (3, 0), (0, 1), (2, 0), (1, 1), (3, 1), (2, 1))
AHEAD = (0, 1, 3, 2)


def drain(ref, sem):
    pltpu.make_async_copy(ref, ref, sem).wait()


def kernel(
    act, basis, grads, first, second,
    update, new_first, new_second,
    act_v, basis_v, grads_v, first_v, second_v,
    mixed_v, picked, proj, table, part, got, held, rows_v, total, update_v, first_o, second_o,
    in_sem, og_sem, a1_send, a1_recv, fw_send, fw_recv, sib_sem, a2_send, a2_recv,
    b_send, b_recv, c_send, c_recv, cs_recv, cf_send, cf_recv, out_sem,
):
    i, j = lax.axis_index("dp"), lax.axis_index("tensor")
    core, chip = i % 2, i // 2
    y, x = chip // 2, chip % 2
    quad, member = j // 4, j % 4
    depth = basis.shape[0]
    width = grads.shape[1]
    half = width // 2

    def chip_at(dy, dx):
        return ((y + dy) % 4) * 2 + (x + dx) % 2

    sibling = (2 * chip + (1 - core), j)
    peers = [(2 * dy + dx, chip_at(dy, dx)) for dy, dx in NEAR]

    loads = [pltpu.make_async_copy(basis, basis_v, in_sem.at[0])]
    loads.append(pltpu.make_async_copy(grads, grads_v.at[core], in_sem.at[1]))
    loads.append(pltpu.make_async_copy(first, first_v, in_sem.at[2]))
    loads.append(pltpu.make_async_copy(second, second_v, in_sem.at[3]))
    for load in loads:
        load.start()
    for b in range(16):
        pltpu.make_async_copy(act.at[:, pl.ds(b * depth, depth)], act_v.at[b], in_sem.at[4]).start()

    barrier = pltpu.get_barrier_semaphore()
    greeted = [sibling] + [(2 * q + core, j) for _, q in peers]
    for k, ahead in enumerate(AHEAD):
        for r in range(4):
            if k or r:
                greeted.append((i, 4 * ((quad + 4 - ahead) % 4) + (member + r) % 4))
    for device in greeted:
        pl.semaphore_signal(barrier, inc=1, device_id=device, device_id_type=MESH)

    loads[0].wait()
    r = lax.broadcasted_iota(jnp.int32, (32, 512), 0)
    col = lax.broadcasted_iota(jnp.int32, (32, 512), 1)
    owner = 2 * (2 * member + ((r >> 3) & 1)) + (r >> 4)
    pick = (col == 32 * owner + 8 * quad + (r & 7)).astype(bf16)
    nt = (((1,), (1,)), ((), ()))
    picked[0, 0] = lax.dot_general(pick, basis_v[...], nt, preferred_element_type=f32).astype(bf16)

    pl.semaphore_wait(barrier, len(greeted))

    for d, q in peers:
        pltpu.make_async_remote_copy(
            picked.at[0, 0], picked.at[0, d], a1_send, a1_recv.at[d], (2 * q + core, j), MESH
        ).start()
    pltpu.make_async_remote_copy(
        picked.at[0, 0], picked.at[1, 0], fw_send, fw_recv.at[0], sibling, MESH
    ).start()
    to_sibling = pltpu.make_async_remote_copy(
        grads, grads_v.at[core], og_sem.at[0], og_sem.at[1], sibling, MESH
    )
    to_sibling.start()

    row = lax.broadcasted_iota(jnp.int32, (512, 512), 0)
    s = lax.broadcasted_iota(jnp.int32, (512, 512), 1)
    kk, pr, d, r = s >> 8, (s >> 7) & 1, (s >> 4) & 7, s & 15
    from_y = (y + 4 - (d >> 1)) & 3
    from_x = (x + 2 - (d & 1)) & 1
    from_core = (core + pr) & 1
    k = 2 * kk + (r >> 3)
    ahead = jnp.where(k == 2, 3, jnp.where(k == 3, 2, k))
    col = 32 * (2 * (2 * from_y + from_x) + from_core) + 8 * ((quad + ahead) & 3) + (r & 7)
    mix = (row == col).astype(bf16)
    mixed_v[...] = jnp.dot(basis_v[...], mix, preferred_element_type=f32).astype(bf16)

    pltpu.make_async_copy(act_v, act_v, in_sem.at[4]).wait()

    def times(pr, d, dy, dx):
        from_chip = ((y + 4 - dy) % 4) * 2 + (x + 2 - dx) % 2
        block = 2 * from_chip + (core + pr) % 2
        return lax.dot_general(picked[pr, d], act_v[block], nt, preferred_element_type=f32)

    acc = times(0, 0, 0, 0)
    for dy, dx in NEAR:
        d = 2 * dy + dx
        drain(picked.at[0, d], a1_recv.at[d])
        pltpu.make_async_remote_copy(
            picked.at[0, d], picked.at[1, d], fw_send, fw_recv.at[d], sibling, MESH
        ).start()
        acc += times(0, d, dy, dx)
    for dy, dx in ((0, 0),) + NEAR:
        d = 2 * dy + dx
        drain(picked.at[1, d], fw_recv.at[d])
        acc += times(1, d, dy, dx)
    acc = acc.astype(bf16)
    proj[0] = acc[:16]
    proj[1] = acc[16:]

    swap = pltpu.make_async_remote_copy(
        proj.at[1 - core], table.at[0, member, core], sib_sem.at[0], sib_sem.at[1], sibling, MESH
    )
    swap.start()
    table[0, member, core] = proj[core]
    drain(table.at[0, member, 1 - core], sib_sem.at[1])
    for k, ahead in enumerate(AHEAD):
        for r in range(4):
            if k or r:
                target = 4 * ((quad + 4 - ahead) % 4) + (member + r) % 4
                pltpu.make_async_remote_copy(
                    table.at[0, member], table.at[k, member], a2_send.at[k], a2_recv.at[k],
                    (i, target), MESH,
                ).start()
    loads[1].wait()
    loads[2].wait()
    loads[3].wait()
    drain(grads_v.at[1 - core], og_sem.at[1])

    def partial(k):
        drain(table.at[k] if k else table.at[0, pl.ds(0, 3)], a2_recv.at[k])
        left = table[k, :, 0].reshape(64, depth)
        right = table[k, :, 1].reshape(64, depth)
        halves = []
        for h in range(2):
            cols = pl.ds(h * half, half)
            halves.append(
                jnp.dot(left, grads_v[0, :, cols], preferred_element_type=f32)
                + jnp.dot(right, grads_v[1, :, cols], preferred_element_type=f32)
            )
        for q in range(8):
            both = [v[8 * q : 8 * q + 8] for v in halves]
            part[k, q] = jnp.concatenate(both, axis=0).astype(bf16)
        for d, q in peers:
            pltpu.make_async_remote_copy(
                part.at[k, q], got.at[k, d - 1], b_send.at[k], b_recv.at[k], (2 * q + core, j), MESH
            ).start()

    def reduce(k):
        drain(got.at[k], b_recv.at[k])
        low = part[k, chip].astype(f32)
        for d in range(7):
            low += got[k, d].astype(f32)
        at = pl.ds(pl.multiple_of(8 * ((quad + AHEAD[k]) % 4), 8), 8)
        for h in range(2):
            cols = pl.ds(h * half, half)
            g = low[8 * h : 8 * h + 8]
            nf = beta_one * first_v[at, cols] + (1.0 - beta_one) * g
            ns = beta_two * second_v[at, cols] + (1.0 - beta_two) * g * g
            first_o[at, cols] = nf
            second_o[at, cols] = ns
            rows_v[pl.ds(8 * (k % 2), 8), cols] = nf / first_fix / (
                jnp.sqrt(ns / second_fix) + adam_eps
            )

    def spread(kk):
        held[kk, 0, 0] = rows_v[...].astype(bf16)
        for d, q in peers:
            pltpu.make_async_remote_copy(
                held.at[kk, 0, 0], held.at[kk, 0, d], c_send.at[kk], c_recv.at[kk],
                (2 * q + core, j), MESH,
            ).start()
        pltpu.make_async_remote_copy(
            held.at[kk, 0, 0], held.at[kk, 1, 0], cf_send.at[kk], cs_recv.at[kk], sibling, MESH
        ).start()

    def forward(kk):
        others = pl.ds(1, 7)
        drain(held.at[kk, 0, others], c_recv.at[kk])
        pltpu.make_async_remote_copy(
            held.at[kk, 0, others], held.at[kk, 1, others], cf_send.at[kk], cf_recv.at[kk],
            sibling, MESH,
        ).start()

    def arrived(kk):
        drain(held.at[kk, 1, 0], cs_recv.at[kk])
        drain(held.at[kk, 1, pl.ds(1, 7)], cf_recv.at[kk])

    partial(0)
    partial(1)
    reduce(0)
    partial(2)
    reduce(1)
    spread(0)
    partial(3)
    reduce(2)
    forward(0)
    reduce(3)
    spread(1)
    outs = [
        pltpu.make_async_copy(first_o, new_first, out_sem.at[0]),
        pltpu.make_async_copy(second_o, new_second, out_sem.at[1]),
    ]
    for out in outs:
        out.start()
    arrived(0)
    tiles = [pl.ds(t * 256, 256) for t in range(width // 256)]
    for cols in tiles:
        total[:, cols] = jnp.dot(
            mixed_v[:, pl.ds(0, 256)], held[0, :, :, :, cols].reshape(256, 256),
            preferred_element_type=f32,
        )
    forward(1)
    arrived(1)
    for t, cols in enumerate(tiles):
        last = jnp.dot(
            mixed_v[:, pl.ds(256, 256)], held[1, :, :, :, cols].reshape(256, 256),
            preferred_element_type=f32,
        )
        update_v[:, cols] = (total[:, cols] + last).astype(bf16)
        out = pltpu.make_async_copy(update_v.at[:, cols], update.at[:, cols], out_sem.at[2 + t])
        out.start()
        outs.append(out)

    drain(picked.at[0, pl.ds(0, 7)], a1_send)
    drain(picked.at[1], fw_send)
    drain(grads, og_sem.at[0])
    drain(proj.at[0], sib_sem.at[0])
    for k in range(4):
        drain(table.at[k] if k else table.at[0, pl.ds(0, 3)], a2_send.at[k])
        drain(got.at[k], b_send.at[k])
    for kk in range(2):
        drain(held.at[kk, 0, pl.ds(1, 7)], c_send.at[kk])
        drain(held.at[kk, 1], cf_send.at[kk])
    for out in outs:
        out.wait()


def on_device(act, basis, grads, first, second):
    tokens, depth = act.shape[0], basis.shape[0]
    rank, width = basis.shape[1], grads.shape[1]
    rows = first.shape[0]
    dma = pltpu.SemaphoreType.DMA
    anywhere = pl.BlockSpec(memory_space=pl.ANY)
    return pl.pallas_call(
        kernel,
        out_shape=(
            jax.ShapeDtypeStruct((depth, width), bf16),
            jax.ShapeDtypeStruct((rows, width), f32),
            jax.ShapeDtypeStruct((rows, width), f32),
        ),
        in_specs=[anywhere] * 5,
        out_specs=[anywhere] * 3,
        scratch_shapes=[
            pltpu.VMEM((16, tokens, depth), bf16),
            pltpu.VMEM((depth, rank), bf16),
            pltpu.VMEM((2, tokens, width), bf16),
            pltpu.VMEM((rows, width), f32),
            pltpu.VMEM((rows, width), f32),
            pltpu.VMEM((depth, rank), bf16),
            pltpu.VMEM((2, 8, 32, depth), bf16),
            pltpu.VMEM((2, 16, tokens), bf16),
            pltpu.VMEM((4, 4, 2, 16, tokens), bf16),
            pltpu.VMEM((4, 8, 16, width // 2), bf16),
            pltpu.VMEM((4, 7, 16, width // 2), bf16),
            pltpu.VMEM((2, 2, 8, 16, width), bf16),
            pltpu.VMEM((16, width), f32),
            pltpu.VMEM((depth, width), f32),
            pltpu.VMEM((depth, width), bf16),
            pltpu.VMEM((rows, width), f32),
            pltpu.VMEM((rows, width), f32),
            dma((5,)), dma((2,)), dma, dma((8,)), dma, dma((8,)), dma((2,)), dma((4,)), dma((4,)),
            dma((4,)), dma((4,)), dma((2,)), dma((2,)), dma((2,)), dma((2,)), dma((2,)),
            dma((2 + width // 256,)),
        ],
        compiler_params=pltpu.CompilerParams(
            collective_id=0, has_side_effects=True, vmem_limit_bytes=48 << 20
        ),
    )(act, basis, grads, first, second)


def solution(mesh):
    placed = (P("dp", None), P("dp", None), P("dp", "tensor"), P("dp", "tensor"), P("dp", "tensor"))
    return jax.shard_map(
        on_device,
        mesh=mesh,
        in_specs=placed,
        out_specs=(P("dp", "tensor"), P("dp", "tensor"), P("dp", "tensor")),
        check_vma=False,
    )
```

```python
import jax
import jax.numpy as jnp
from jax import lax
from jax.experimental import pallas as pl
from jax.experimental.pallas import tpu as pltpu
from jax.sharding import PartitionSpec as P

beta_one = 0.9
beta_two = 0.999
first_fix = 1.0 - 0.9**50
second_fix = 1.0 - 0.999**50
adam_eps = 1e-08

MESH = pl.DeviceIdType.MESH
bf16 = jnp.bfloat16
f32 = jnp.float32
scope = jax.named_scope

NEAR = ((1, 0), (3, 0), (0, 1), (2, 0), (1, 1), (3, 1), (2, 1))
AHEAD = (0, 1, 3, 2)
NT = (((1,), (1,)), ((), ()))


def drain(ref, sem):
    pltpu.make_async_copy(ref, ref, sem).wait()


def exchange(
    act, basis, grads, first, second,
    held, mixed, first_o, second_o,
    act_v, basis_v, grads_v, first_v, second_v,
    mixed_v, picked, proj, table, part, got, send_v, new_first, new_second,
    in_sem, og_sem, a1_send, a1_recv, fw_send, fw_recv, sib_sem, a2_send, a2_recv,
    b_send, b_recv, c_send, c_recv, cs_recv, cf_send, cf_recv, out_sem,
):
    i, j = lax.axis_index("dp"), lax.axis_index("tensor")
    core, chip = i % 2, i // 2
    y, x = chip // 2, chip % 2
    quad, member = j // 4, j % 4
    depth = basis.shape[0]
    half = grads.shape[1] // 2
    twin = 2 * chip + (1 - core)

    sibling = (twin, j)
    peers = [(2 * dy + dx, ((y + dy) % 4) * 2 + (x + dx) % 2) for dy, dx in NEAR]

    barrier = pltpu.get_barrier_semaphore()
    greeted = [sibling] + [(2 * q + core, j) for _, q in peers]
    for k, ahead in enumerate(AHEAD):
        for r in range(4):
            if k or r:
                greeted.append((i, 4 * ((quad + 4 - ahead) % 4) + (member + r) % 4))
    for r in range(1, 4):
        greeted.append((twin, 4 * quad + (member + r) % 4))
    for device in greeted:
        pl.semaphore_signal(barrier, inc=1, device_id=device, device_id_type=MESH)

    loads = [
        pltpu.make_async_copy(basis, basis_v, in_sem.at[0]),
        pltpu.make_async_copy(grads, grads_v.at[core], in_sem.at[1]),
        pltpu.make_async_copy(first, first_v, in_sem.at[2]),
        pltpu.make_async_copy(second, second_v, in_sem.at[3]),
    ]
    loads[0].start()
    for b in range(16):
        pltpu.make_async_copy(act.at[:, pl.ds(b * depth, depth)], act_v.at[b], in_sem.at[4]).start()
    for load in loads[1:]:
        load.start()

    loads[0].wait()
    r = lax.broadcasted_iota(jnp.int32, (32, 512), 0)
    col = lax.broadcasted_iota(jnp.int32, (32, 512), 1)
    owner = 2 * (2 * member + ((r >> 3) & 1)) + (r >> 4)
    pick = (col == 32 * owner + 8 * quad + (r & 7)).astype(bf16)
    picked[0, 0] = lax.dot_general(pick, basis_v[...], NT, preferred_element_type=f32).astype(bf16)

    with scope("greet"):
        pl.semaphore_wait(barrier, len(greeted))

    with scope("send_columns"):
        for d, q in peers:
            pltpu.make_async_remote_copy(
                picked.at[0, 0], picked.at[0, d], a1_send, a1_recv.at[d], (2 * q + core, j), MESH
            ).start()
        pltpu.make_async_remote_copy(
            picked.at[0, 0], picked.at[1, 0], fw_send, fw_recv.at[0], sibling, MESH
        ).start()
        pltpu.make_async_remote_copy(
            grads, grads_v.at[core], og_sem.at[0], og_sem.at[1], sibling, MESH
        ).start()

    with scope("reorder_basis"):
        row = lax.broadcasted_iota(jnp.int32, (512, 512), 0)
        s = lax.broadcasted_iota(jnp.int32, (512, 512), 1)
        k, pr, d, r = s >> 7, (s >> 6) & 1, (s >> 3) & 7, s & 7
        from_y = (y + 4 - (d >> 1)) & 3
        from_x = (x + 2 - (d & 1)) & 1
        from_core = (core + pr) & 1
        ahead = jnp.where(k == 2, 3, jnp.where(k == 3, 2, k))
        col = 32 * (2 * (2 * from_y + from_x) + from_core) + 8 * ((quad + ahead) & 3) + r
        mix = (row == col).astype(bf16)
        mixed_v[...] = jnp.dot(basis_v[...], mix, preferred_element_type=f32).astype(bf16)
        mixed_out = pltpu.make_async_copy(mixed_v, mixed, out_sem.at[0])
        mixed_out.start()

    with scope("act_wait"):
        pltpu.make_async_copy(act_v, act_v, in_sem.at[4]).wait()

    def times(pr, dy, dx):
        from_chip = ((y + 4 - dy) % 4) * 2 + (x + 2 - dx) % 2
        block = 2 * from_chip + (core + pr) % 2
        return lax.dot_general(
            picked[pr, 2 * dy + dx], act_v[block], NT, preferred_element_type=f32
        )

    def from_sibling(acc, dy, dx):
        with scope("sibling_columns"):
            drain(picked.at[1, 2 * dy + dx], fw_recv.at[2 * dy + dx])
        return acc + times(1, dy, dx)

    behind = ((0, 0),) + NEAR
    acc = times(0, 0, 0)
    for t, (dy, dx) in enumerate(NEAR):
        d = 2 * dy + dx
        with scope("columns%d" % t):
            drain(picked.at[0, d], a1_recv.at[d])
        pltpu.make_async_remote_copy(
            picked.at[0, d], picked.at[1, d], fw_send, fw_recv.at[d], sibling, MESH
        ).start()
        acc += times(0, dy, dx)
        if t:
            acc = from_sibling(acc, *behind[t - 1])
    acc = from_sibling(acc, *behind[6])
    acc = from_sibling(acc, *behind[7])
    acc = acc.astype(bf16)
    proj[0] = acc[:16]
    proj[1] = acc[16:]

    with scope("send_projected"):
        pltpu.make_async_remote_copy(
            proj.at[1 - core], table.at[0, member, core], sib_sem.at[0], sib_sem.at[1], sibling, MESH
        ).start()
        for r in range(1, 4):
            target = 4 * quad + (member + r) % 4
            for to_core, to_dp in ((core, i), (1 - core, twin)):
                pltpu.make_async_remote_copy(
                    proj.at[to_core], table.at[0, member, core], a2_send.at[0], a2_recv.at[0],
                    (to_dp, target), MESH,
                ).start()
        table[0, member, core] = proj[core]
        drain(table.at[0, member, 1 - core], sib_sem.at[1])
        for k, ahead in enumerate(AHEAD):
            for r in range(4):
                if k:
                    target = 4 * ((quad + 4 - ahead) % 4) + (member + r) % 4
                    pltpu.make_async_remote_copy(
                        table.at[0, member], table.at[k, member], a2_send.at[k], a2_recv.at[k],
                        (i, target), MESH,
                    ).start()
    for load in loads[1:]:
        load.wait()
    drain(grads_v.at[1 - core], og_sem.at[1])

    def partial(k):
        with scope("wait_projected%d" % k):
            drain(table.at[k] if k else table.at[0, pl.ds(0, 3)], a2_recv.at[k])
        with scope("partial%d" % k):
            left = table[k, :, 0].reshape(64, depth)
            right = table[k, :, 1].reshape(64, depth)
            halves = []
            for h in range(2):
                cols = pl.ds(h * half, half)
                halves.append(
                    jnp.dot(left, grads_v[0, :, cols], preferred_element_type=f32)
                    + jnp.dot(right, grads_v[1, :, cols], preferred_element_type=f32)
                )
            for q in range(8):
                both = [v[8 * q : 8 * q + 8] for v in halves]
                part[k, q] = jnp.concatenate(both, axis=0).astype(bf16)
            for d, q in peers:
                pltpu.make_async_remote_copy(
                    part.at[k, q], got.at[k, d - 1], b_send.at[k], b_recv.at[k],
                    (2 * q + core, j), MESH,
                ).start()

    def reduce(k):
        with scope("wait_sums%d" % k):
            drain(got.at[k], b_recv.at[k])
        with scope("adam%d" % k):
            low = part[k, chip].astype(f32)
            for d in range(7):
                low += got[k, d].astype(f32)
            at = pl.ds(pl.multiple_of(8 * ((quad + AHEAD[k]) % 4), 8), 8)
            rows = []
            for h in range(2):
                cols = pl.ds(h * half, half)
                g = low[8 * h : 8 * h + 8]
                nf = beta_one * first_v[at, cols] + (1.0 - beta_one) * g
                ns = beta_two * second_v[at, cols] + (1.0 - beta_two) * g * g
                new_first[at, cols] = nf
                new_second[at, cols] = ns
                rows.append(nf / first_fix / (jnp.sqrt(ns / second_fix) + adam_eps))
            send_v[k] = jnp.concatenate(rows, axis=0).astype(bf16)
            for d, q in peers:
                pltpu.make_async_remote_copy(
                    send_v.at[k], held.at[k, 0, d], c_send.at[k], c_recv.at[k],
                    (2 * q + core, j), MESH,
                ).start()
            pltpu.make_async_remote_copy(
                send_v.at[k], held.at[k, 1, 0], cf_send.at[k], cs_recv.at[k], sibling, MESH
            ).start()
            pltpu.make_async_copy(send_v.at[k], held.at[k, 0, 0], out_sem.at[1]).start()

    def forward(k):
        others = pl.ds(1, 7)
        with scope("wait_rows%d" % k):
            drain(held.at[k, 0, others], c_recv.at[k])
        pltpu.make_async_remote_copy(
            held.at[k, 0, others], held.at[k, 1, others], cf_send.at[k], cf_recv.at[k],
            sibling, MESH,
        ).start()


    partial(0)
    partial(1)
    reduce(0)
    partial(2)
    reduce(1)
    partial(3)
    reduce(2)
    reduce(3)
    outs = [
        mixed_out,
        pltpu.make_async_copy(new_first, first_o, out_sem.at[2]),
        pltpu.make_async_copy(new_second, second_o, out_sem.at[3]),
    ]
    for out in outs[1:]:
        out.start()
    for k in range(4):
        forward(k)

    drain(picked.at[0, pl.ds(0, 7)], a1_send)
    drain(picked.at[1], fw_send)
    drain(grads, og_sem.at[0])
    drain(proj.at[0], sib_sem.at[0])
    for k in range(4):
        drain(table.at[k] if k else table.at[0, pl.ds(0, 3)], a2_send.at[k])
        drain(got.at[k], b_send.at[k])
        drain(held.at[k, 0, pl.ds(1, 7)], c_send.at[k])
        drain(held.at[k, 1], cf_send.at[k])
    for out in outs:
        out.wait()
    drain(send_v, out_sem.at[1])
    with scope("wait_sibling_rows"):
        for k in range(4):
            drain(held.at[k, 1, 0], cs_recv.at[k])
            drain(held.at[k, 1, pl.ds(1, 7)], cf_recv.at[k])


def finish(held, mixed, first_i, second_i, update, first_o, second_o, rows_v, update_v, sem):
    outs = [
        pltpu.make_async_copy(first_i, first_o, sem.at[0]),
        pltpu.make_async_copy(second_i, second_o, sem.at[1]),
    ]
    for out in outs:
        out.start()
    width = update.shape[1]
    half = width // 2
    done = 0
    for h in range(2):
        for k in range(4):
            rows = held[k].reshape(16, 16, half).astype(f32)[:, 8 * h : 8 * h + 8]
            rows_v[128 * k : 128 * k + 128, pl.ds(h * half, half)] = rows.reshape(128, half).astype(bf16)
        while done < width and done + 256 <= (h + 1) * half:
            cols = pl.ds(done, 256)
            update_v[:, cols] = jnp.dot(
                mixed[...], rows_v[:, cols], preferred_element_type=f32
            ).astype(bf16)
            out = pltpu.make_async_copy(update_v.at[:, cols], update.at[:, cols], sem.at[2 + done // 256])
            out.start()
            outs.append(out)
            done += 256
    for out in outs:
        out.wait()


def on_device(act, basis, grads, first, second):
    tokens, depth = act.shape[0], basis.shape[0]
    rank, width = basis.shape[1], grads.shape[1]
    rows = first.shape[0]
    half = width // 2
    dma = pltpu.SemaphoreType.DMA
    anywhere = pl.BlockSpec(memory_space=pl.ANY)
    in_vmem = pl.BlockSpec(memory_space=pltpu.VMEM)
    operands = [pltpu.with_memory_space_constraint(v, pltpu.HBM) for v in (act, basis, grads, first, second)]
    held, mixed, new_first, new_second = pl.pallas_call(
        exchange,
        out_shape=(
            pltpu.VMEM((4, 2, 8, 16, half), bf16),
            pltpu.VMEM((depth, rank), bf16),
            pltpu.VMEM((rows, width), f32),
            pltpu.VMEM((rows, width), f32),
        ),
        in_specs=[anywhere] * 5,
        out_specs=[anywhere] * 4,
        scratch_shapes=[
            pltpu.VMEM((16, tokens, depth), bf16),
            pltpu.VMEM((depth, rank), bf16),
            pltpu.VMEM((2, tokens, width), bf16),
            pltpu.VMEM((rows, width), f32),
            pltpu.VMEM((rows, width), f32),
            pltpu.VMEM((depth, rank), bf16),
            pltpu.VMEM((2, 8, 32, depth), bf16),
            pltpu.VMEM((2, 16, tokens), bf16),
            pltpu.VMEM((4, 4, 2, 16, tokens), bf16),
            pltpu.VMEM((4, 8, 16, half), bf16),
            pltpu.VMEM((4, 7, 16, half), bf16),
            pltpu.VMEM((4, 16, half), bf16),
            pltpu.VMEM((rows, width), f32),
            pltpu.VMEM((rows, width), f32),
            dma((5,)), dma((2,)), dma, dma((8,)), dma, dma((8,)), dma((2,)), dma((4,)), dma((4,)),
            dma((4,)), dma((4,)), dma((4,)), dma((4,)), dma((4,)), dma((4,)), dma((4,)),
            dma((4,)),
        ],
        compiler_params=pltpu.CompilerParams(
            collective_id=0, has_side_effects=True, vmem_limit_bytes=32 << 20
        ),
    )(*operands)
    return pl.pallas_call(
        finish,
        out_shape=(
            pltpu.HBM((depth, width), bf16),
            pltpu.HBM((rows, width), f32),
            pltpu.HBM((rows, width), f32),
        ),
        in_specs=[in_vmem, in_vmem, anywhere, anywhere],
        out_specs=[anywhere] * 3,
        scratch_shapes=[
            pltpu.VMEM((rank, width), bf16),
            pltpu.VMEM((depth, width), bf16),
            dma((2 + width // 256,)),
        ],
        compiler_params=pltpu.CompilerParams(vmem_limit_bytes=24 << 20),
    )(held, mixed, new_first, new_second)


def solution(mesh):
    placed = (P("dp", None), P("dp", None), P("dp", "tensor"), P("dp", "tensor"), P("dp", "tensor"))
    return jax.shard_map(
        on_device,
        mesh=mesh,
        in_specs=placed,
        out_specs=(P("dp", "tensor"), P("dp", "tensor"), P("dp", "tensor")),
        check_vma=False,
    )
```

```python
import jax
import jax.numpy as jnp
from jax import lax
from jax.experimental import pallas as pl
from jax.experimental.pallas import tpu as pltpu
from jax.sharding import PartitionSpec as P

beta_one = 0.9
beta_two = 0.999
first_fix = 1.0 - 0.9**50
second_fix = 1.0 - 0.999**50
adam_eps = 1e-08

MESH = pl.DeviceIdType.MESH
bf16 = jnp.bfloat16
f32 = jnp.float32
scope = jax.named_scope

NEAR = ((1, 0), (3, 0), (0, 1), (2, 0), (1, 1), (3, 1), (2, 1))
ALL = ((0, 0),) + NEAR
RELAY = ("y then x", "x then y", "y then x", None)
NT = (((1,), (1,)), ((), ()))


def drain(ref, sem):
    pltpu.make_async_copy(ref, ref, sem).wait()


def slot_sem(d):
    return 0 if d < 4 else 1 if d == 4 else 2


def exchange(
    act, basis, grads, first, second,
    held, mixed, first_o, second_o,
    act_v, basis_v, grads_v, first_v, second_v,
    mixed_v, picked, proj, table, part, got, send_v, total, new_first, new_second,
    in_sem, og_sem, a1_send, a1_recv, fw_send, fw_recv, sib_sem, a2_send, a2_recv,
    b_send, b_recv, c_send, c_recv, cs_recv, cf_send, cf_recv, out_sem,
):
    i, j = lax.axis_index("dp"), lax.axis_index("tensor")
    core, chip = i % 2, i // 2
    y, x = chip // 2, chip % 2
    z, lo = j // 2, j % 2
    pair, odd = (z // 2) % 2, z % 2
    member = 2 * odd + lo
    depth = basis.shape[0]
    half = grads.shape[1] // 2
    twin = 2 * chip + (1 - core)

    sibling = (twin, j)
    peers = [(4 * dx + dy, ((y + dy) % 4) * 2 + (x + dx) % 2) for dy, dx in NEAR]
    by_slot = dict(peers)

    loads = [
        pltpu.make_async_copy(basis, basis_v, in_sem.at[0]),
        pltpu.make_async_copy(grads, grads_v.at[core], in_sem.at[1]),
        pltpu.make_async_copy(first, first_v, in_sem.at[2]),
        pltpu.make_async_copy(second, second_v, in_sem.at[3]),
    ]
    loads[0].start()

    barrier = pltpu.get_barrier_semaphore()
    def at(dz, to_lo):
        return 2 * ((z + 8 + dz) % 8) + to_lo

    mates = [at(0, 1 - lo), at(1 - 2 * odd, 0), at(1 - 2 * odd, 1)]
    next_z, across = 2 * odd - 1, 4 * lo - 2
    greeted = [sibling] + [(2 * q + core, j) for _, q in peers]
    greeted += [(to_dp, mate) for mate in mates for to_dp in (i, twin)]
    greeted += [(i, at(next_z, 0)), (i, at(next_z, 1)), (i, at(2, 0)), (i, at(-2, 1))]
    for device in greeted:
        pl.semaphore_signal(barrier, inc=1, device_id=device, device_id_type=MESH)

    loads[0].wait()
    r = lax.broadcasted_iota(jnp.int32, (64, 512), 0)
    col = lax.broadcasted_iota(jnp.int32, (64, 512), 1)
    owner = 2 * (2 * member + ((r >> 3) & 1)) + ((r >> 4) & 1)
    pick = (col == 32 * owner + 8 * (2 * (r >> 5) + pair) + (r & 7)).astype(bf16)
    both = lax.dot_general(pick, basis_v[...], NT, preferred_element_type=f32).astype(bf16)
    picked[0, 0, 0] = both[:32]
    picked[1, 0, 0] = both[32:]

    with scope("greet"):
        pl.semaphore_wait(barrier, len(greeted))

    def send_columns(t):
        with scope("send_columns%d" % t):
            for d, q in peers:
                pltpu.make_async_remote_copy(
                    picked.at[t, 0, 0], picked.at[t, 0, d], a1_send.at[t], a1_recv.at[8 if t else d],
                    (2 * q + core, j), MESH,
                ).start()
            pltpu.make_async_remote_copy(
                picked.at[t, 0, 0], picked.at[t, 1, 0], fw_send.at[t], fw_recv.at[8 * t], sibling, MESH
            ).start()

    send_columns(0)
    for b in range(16):
        pltpu.make_async_copy(act.at[:, pl.ds(b * depth, depth)], act_v.at[b], in_sem.at[4]).start()
    for load in loads[1:]:
        load.start()
    pltpu.make_async_remote_copy(
        grads, grads_v.at[core], og_sem.at[0], og_sem.at[1], sibling, MESH
    ).start()

    with scope("reorder_basis"):
        row = lax.broadcasted_iota(jnp.int32, (512, 512), 0)
        s = lax.broadcasted_iota(jnp.int32, (512, 512), 1)
        k, pr, d, r = s >> 7, (s >> 6) & 1, (s >> 3) & 7, s & 7
        from_y = (y + 4 - (d & 3)) & 3
        from_x = (x + 2 - (d >> 2)) & 1
        from_core = (core + pr) & 1
        block = 2 * (k >> 1) + ((pair + k) & 1)
        col = 32 * (2 * (2 * from_y + from_x) + from_core) + 8 * block + r
        mix = (row == col).astype(bf16)
        mixed_v[...] = jnp.dot(basis_v[...], mix, preferred_element_type=f32).astype(bf16)
        mixed_out = pltpu.make_async_copy(mixed_v, mixed, out_sem.at[0])
        mixed_out.start()

    with scope("act_wait"):
        pltpu.make_async_copy(act_v, act_v, in_sem.at[4]).wait()

    def partial(k):
        with scope("wait_projected%d" % k):
            drain(table.at[k] if k % 2 else table.at[k, pl.ds(0, 3)], a2_recv.at[k])
        with scope("partial%d" % k):
            left = table[k, :, 0].reshape(64, depth)
            right = table[k, :, 1].reshape(64, depth)
            halves = []
            for h in range(2):
                cols = pl.ds(h * half, half)
                halves.append(
                    jnp.dot(left, grads_v[0, :, cols], preferred_element_type=f32)
                    + jnp.dot(right, grads_v[1, :, cols], preferred_element_type=f32)
                )
            for q in range(8):
                both = [v[8 * q : 8 * q + 8] for v in halves]
                part[k, q] = jnp.concatenate(both, axis=0).astype(bf16)
            for d, q in peers:
                pltpu.make_async_remote_copy(
                    part.at[k, q], got.at[k, d - 1], b_send.at[k], b_recv.at[k],
                    (2 * q + core, j), MESH,
                ).start()

    def times(t, pr, dy, dx):
        from_chip = ((y + 4 - dy) % 4) * 2 + (x + 2 - dx) % 2
        block = 2 * from_chip + (core + pr) % 2
        return lax.dot_general(
            picked[t, pr, 4 * dx + dy], act_v[block], NT, preferred_element_type=f32
        )

    def arrive(n):
        d = NEAR[n][0] + 4 * NEAR[n][1]
        with scope("columns0_%d" % n):
            drain(picked.at[0, 0, d], a1_recv.at[d])
        pltpu.make_async_remote_copy(
            picked.at[0, 0, d], picked.at[0, 1, d], fw_send.at[0], fw_recv.at[d], sibling, MESH
        ).start()

    def sibling_arrive(n):
        d = ALL[n][0] + 4 * ALL[n][1]
        with scope("sibling_columns0"):
            drain(picked.at[0, 1, d], fw_recv.at[d])

    def to_mates(t, acc):
        with scope("to_mates%d" % t):
            k = 2 * t
            acc = acc.astype(bf16)
            proj[t, 0] = acc[:16]
            proj[t, 1] = acc[16:]
            pltpu.make_async_remote_copy(
                proj.at[t, 1 - core], table.at[k, member, core], sib_sem.at[t, 0], sib_sem.at[t, 1],
                sibling, MESH,
            ).start()
            for mate in mates:
                for to_core, to_dp in ((core, i), (1 - core, twin)):
                    pltpu.make_async_remote_copy(
                        proj.at[t, to_core], table.at[k, member, core], a2_send.at[k], a2_recv.at[k],
                        (to_dp, mate), MESH,
                    ).start()
            table[k, member, core] = proj[t, core]

    def to_others(t):
        with scope("to_others%d" % t):
            k = 2 * t
            drain(table.at[k, member, 1 - core], sib_sem.at[t, 1])
            for dz in (next_z, across):
                for to_lo in (0, 1):
                    pltpu.make_async_remote_copy(
                        table.at[k, member], table.at[k + 1, member], a2_send.at[k + 1],
                        a2_recv.at[k + 1], (i, at(dz, to_lo)), MESH,
                    ).start()

    acc = times(0, 0, 0, 0)
    for n, offset in enumerate(NEAR):
        arrive(n)
        if n == 0:
            send_columns(1)
        acc += times(0, 0, *offset)
        if n:
            sibling_arrive(n - 1)
            acc += times(0, 1, *ALL[n - 1])
    for n in (6, 7):
        sibling_arrive(n)
        acc += times(0, 1, *ALL[n])
    to_mates(0, acc)

    rest = pl.ds(1, 7)
    with scope("columns1"):
        drain(picked.at[1, 0, rest], a1_recv.at[8])
    pltpu.make_async_remote_copy(
        picked.at[1, 0, rest], picked.at[1, 1, rest], fw_send.at[1], fw_recv.at[8], sibling, MESH
    ).start()
    acc = times(1, 0, 0, 0)
    for offset in NEAR:
        acc += times(1, 0, *offset)
    total[...] = acc
    to_others(0)
    with scope("sibling_columns1"):
        drain(picked.at[1, 1], fw_recv.at[8])
    acc = total[...]
    for offset in ALL:
        acc += times(1, 1, *offset)
    to_mates(1, acc)

    for load in loads[1:]:
        load.wait()
    drain(grads_v.at[1 - core], og_sem.at[1])
    partial(0)
    to_others(1)

    def reduce(k):
        with scope("wait_sums%d" % k):
            drain(got.at[k], b_recv.at[k])
        with scope("adam%d" % k):
            low = part[k, chip].astype(f32)
            for d in range(7):
                low += got[k, d].astype(f32)
            mine = pl.ds(pl.multiple_of(8 * (2 * (k // 2) + (pair + k) % 2), 8), 8)
            rows = []
            for h in range(2):
                cols = pl.ds(h * half, half)
                g = low[8 * h : 8 * h + 8]
                nf = beta_one * first_v[mine, cols] + (1.0 - beta_one) * g
                ns = beta_two * second_v[mine, cols] + (1.0 - beta_two) * g * g
                new_first[mine, cols] = nf
                new_second[mine, cols] = ns
                rows.append(nf / first_fix / (jnp.sqrt(ns / second_fix) + adam_eps))
            send_v[k] = jnp.concatenate(rows, axis=0).astype(bf16)
            for d, q in peers:
                if d < 5 or RELAY[k] is None:
                    pltpu.make_async_remote_copy(
                        send_v.at[k], held.at[k, 0, d], c_send.at[k, 0], c_recv.at[k, slot_sem(d)],
                        (2 * q + core, j), MESH,
                    ).start()
            pltpu.make_async_remote_copy(
                send_v.at[k], held.at[k, 1, 0], cf_send.at[k], cs_recv.at[k], sibling, MESH
            ).start()
            pltpu.make_async_copy(send_v.at[k], held.at[k, 0, 0], out_sem.at[1]).start()

    def relay(k):
        if RELAY[k] == "y then x":
            with scope("wait_y_rows%d" % k):
                drain(held.at[k, 0, pl.ds(1, 3)], c_recv.at[k, 0])
            with scope("relay%d" % k):
                pltpu.make_async_remote_copy(
                    held.at[k, 0, pl.ds(1, 3)], held.at[k, 0, pl.ds(5, 3)], c_send.at[k, 1],
                    c_recv.at[k, 2], (2 * by_slot[4] + core, j), MESH,
                ).start()
        if RELAY[k] == "x then y":
            with scope("wait_x_rows%d" % k):
                drain(held.at[k, 0, 4], c_recv.at[k, 1])
            with scope("relay%d" % k):
                for d in (1, 3, 2):
                    pltpu.make_async_remote_copy(
                        held.at[k, 0, 4], held.at[k, 0, 4 + d], c_send.at[k, 1],
                        c_recv.at[k, 2], (2 * by_slot[d] + core, j), MESH,
                    ).start()

    def forward(k):
        with scope("wait_rows%d" % k):
            if RELAY[k] != "y then x":
                drain(held.at[k, 0, pl.ds(1, 3)], c_recv.at[k, 0])
            if RELAY[k] != "x then y":
                drain(held.at[k, 0, 4], c_recv.at[k, 1])
            drain(held.at[k, 0, pl.ds(5, 3)], c_recv.at[k, 2])
        others = pl.ds(1, 7)
        pltpu.make_async_remote_copy(
            held.at[k, 0, others], held.at[k, 1, others], cf_send.at[k], cf_recv.at[k],
            sibling, MESH,
        ).start()

    for k in range(1, 4):
        partial(k)
    reduce(0)
    for t in range(2):
        drain(picked.at[t, 0, pl.ds(0, 7)], a1_send.at[t])
        drain(picked.at[t, 1], fw_send.at[t])
        drain(proj.at[t, 0], sib_sem.at[t, 0])
    drain(grads, og_sem.at[0])
    reduce(1)
    for k in range(4):
        drain(table.at[k] if k % 2 else table.at[k, pl.ds(0, 3)], a2_send.at[k])
    reduce(2)
    relay(0)
    reduce(3)
    relay(1)
    relay(2)
    relay(3)
    for k in range(4):
        drain(got.at[k], b_send.at[k])
    outs = [
        mixed_out,
        pltpu.make_async_copy(new_first, first_o, out_sem.at[2]),
        pltpu.make_async_copy(new_second, second_o, out_sem.at[3]),
    ]
    for out in outs[1:]:
        out.start()
    for k in range(4):
        forward(k)

    for k in range(4):
        if RELAY[k] is None:
            drain(held.at[k, 0, pl.ds(1, 7)], c_send.at[k, 0])
        else:
            drain(held.at[k, 0, pl.ds(1, 4)], c_send.at[k, 0])
            drain(held.at[k, 0, pl.ds(5, 3)], c_send.at[k, 1])
        drain(held.at[k, 1], cf_send.at[k])
    for out in outs:
        out.wait()
    drain(send_v, out_sem.at[1])
    with scope("wait_sibling_rows"):
        for k in range(4):
            drain(held.at[k, 1, 0], cs_recv.at[k])
            drain(held.at[k, 1, pl.ds(1, 7)], cf_recv.at[k])


def finish(held, mixed, first_i, second_i, update, first_o, second_o, rows_v, update_v, sem):
    outs = [
        pltpu.make_async_copy(first_i, first_o, sem.at[0]),
        pltpu.make_async_copy(second_i, second_o, sem.at[1]),
    ]
    for out in outs:
        out.start()
    width = update.shape[1]
    half = width // 2
    done = 0
    for h in range(2):
        for k in range(4):
            rows = held[k].reshape(16, 16, half).astype(f32)[:, 8 * h : 8 * h + 8]
            rows_v[128 * k : 128 * k + 128, pl.ds(h * half, half)] = rows.reshape(128, half).astype(bf16)
        while done < width and done + 256 <= (h + 1) * half:
            cols = pl.ds(done, 256)
            update_v[:, cols] = jnp.dot(
                mixed[...], rows_v[:, cols], preferred_element_type=f32
            ).astype(bf16)
            out = pltpu.make_async_copy(update_v.at[:, cols], update.at[:, cols], sem.at[2 + done // 256])
            out.start()
            outs.append(out)
            done += 256
    with scope("results_out"):
        for out in outs:
            out.wait()


def on_device(act, basis, grads, first, second):
    tokens, depth = act.shape[0], basis.shape[0]
    rank, width = basis.shape[1], grads.shape[1]
    rows = first.shape[0]
    half = width // 2
    dma = pltpu.SemaphoreType.DMA
    anywhere = pl.BlockSpec(memory_space=pl.ANY)
    in_vmem = pl.BlockSpec(memory_space=pltpu.VMEM)
    operands = [pltpu.with_memory_space_constraint(v, pltpu.HBM) for v in (act, basis, grads, first, second)]
    held, mixed, new_first, new_second = pl.pallas_call(
        exchange,
        out_shape=(
            pltpu.VMEM((4, 2, 8, 16, half), bf16),
            pltpu.VMEM((depth, rank), bf16),
            pltpu.VMEM((rows, width), f32),
            pltpu.VMEM((rows, width), f32),
        ),
        in_specs=[anywhere] * 5,
        out_specs=[anywhere] * 4,
        scratch_shapes=[
            pltpu.VMEM((16, tokens, depth), bf16),
            pltpu.VMEM((depth, rank), bf16),
            pltpu.VMEM((2, tokens, width), bf16),
            pltpu.VMEM((rows, width), f32),
            pltpu.VMEM((rows, width), f32),
            pltpu.VMEM((depth, rank), bf16),
            pltpu.VMEM((2, 2, 8, 32, depth), bf16),
            pltpu.VMEM((2, 2, 16, tokens), bf16),
            pltpu.VMEM((4, 4, 2, 16, tokens), bf16),
            pltpu.VMEM((4, 8, 16, half), bf16),
            pltpu.VMEM((4, 7, 16, half), bf16),
            pltpu.VMEM((4, 16, half), bf16),
            pltpu.VMEM((32, tokens), f32),
            pltpu.VMEM((rows, width), f32),
            pltpu.VMEM((rows, width), f32),
            dma((5,)), dma((2,)), dma((2,)), dma((9,)), dma((2,)), dma((9,)), dma((2, 2)), dma((4,)), dma((4,)),
            dma((4,)), dma((4,)), dma((4, 2)), dma((4, 3)), dma((4,)), dma((4,)), dma((4,)),
            dma((4,)),
        ],
        compiler_params=pltpu.CompilerParams(
            collective_id=0, has_side_effects=True, vmem_limit_bytes=32 << 20
        ),
    )(*operands)
    return pl.pallas_call(
        finish,
        out_shape=(
            pltpu.HBM((depth, width), bf16),
            pltpu.HBM((rows, width), f32),
            pltpu.HBM((rows, width), f32),
        ),
        in_specs=[in_vmem, in_vmem, anywhere, anywhere],
        out_specs=[anywhere] * 3,
        scratch_shapes=[
            pltpu.VMEM((rank, width), bf16),
            pltpu.VMEM((depth, width), bf16),
            dma((2 + width // 256,)),
        ],
        compiler_params=pltpu.CompilerParams(vmem_limit_bytes=24 << 20),
    )(held, mixed, new_first, new_second)


def solution(mesh):
    placed = (P("dp", None), P("dp", None), P("dp", "tensor"), P("dp", "tensor"), P("dp", "tensor"))
    return jax.shard_map(
        on_device,
        mesh=mesh,
        in_specs=placed,
        out_specs=(P("dp", "tensor"), P("dp", "tensor"), P("dp", "tensor")),
        check_vma=False,
    )
```

```python
import jax
import jax.numpy as jnp
from jax import lax
from jax.experimental import pallas as pl
from jax.experimental.pallas import tpu as pltpu
from jax.sharding import PartitionSpec as P

beta_one = 0.9
beta_two = 0.999
first_fix = 1.0 - 0.9**50
second_fix = 1.0 - 0.999**50
adam_eps = 1e-08

MESH = pl.DeviceIdType.MESH
bf16 = jnp.bfloat16
f32 = jnp.float32
scope = jax.named_scope

NEAR = ((1, 0), (3, 0), (0, 1), (2, 0), (1, 1), (3, 1), (2, 1))
ALL = ((0, 0),) + NEAR
RELAY = ("y then x", "x then y", "y then x", None)
NT = (((1,), (1,)), ((), ()))


def drain(ref, sem):
    pltpu.make_async_copy(ref, ref, sem).wait()


def slot_sem(d):
    return 0 if d < 4 else 1 if d == 4 else 2


def exchange(
    act, basis, grads, first, second,
    held, mixed, early, new_first, new_second,
    act_v, basis_v, grads_v, first_v, second_v,
    picked, proj, table, part, got, total, rows_v,
    in_sem, sent, og_recv, a1_recv, fw_recv, sib_recv, a2_recv, b_recv, c_recv, cf_recv,
):
    i, j = lax.axis_index("dp"), lax.axis_index("tensor")
    core, chip = i % 2, i // 2
    y, x = chip // 2, chip % 2
    z, lo = j // 2, j % 2
    pair, odd = (z // 2) % 2, z % 2
    member = 2 * odd + lo
    depth = basis.shape[0]
    half = grads.shape[1] // 2
    twin = 2 * chip + (1 - core)

    sibling = (twin, j)
    peers = [(4 * dx + dy, ((y + dy) % 4) * 2 + (x + dx) % 2) for dy, dx in NEAR]
    by_slot = dict(peers)

    loads = [
        pltpu.make_async_copy(basis, basis_v, in_sem.at[0]),
        pltpu.make_async_copy(grads, grads_v.at[core], in_sem.at[1]),
        pltpu.make_async_copy(first, first_v, in_sem.at[2]),
        pltpu.make_async_copy(second, second_v, in_sem.at[3]),
    ]
    loads[0].start()

    barrier = pltpu.get_barrier_semaphore()
    def at(dz, to_lo):
        return 2 * ((z + 8 + dz) % 8) + to_lo

    mates = [at(0, 1 - lo), at(1 - 2 * odd, 0), at(1 - 2 * odd, 1)]
    next_z, across = 2 * odd - 1, 4 * lo - 2
    greeted = [sibling] + [(2 * q + core, j) for _, q in peers]
    greeted += [(to_dp, mate) for mate in mates for to_dp in (i, twin)]
    greeted += [(i, at(next_z, 0)), (i, at(next_z, 1)), (i, at(2, 0)), (i, at(-2, 1))]
    for device in greeted:
        pl.semaphore_signal(barrier, inc=1, device_id=device, device_id_type=MESH)

    loads[0].wait()
    r = lax.broadcasted_iota(jnp.int32, (64, 512), 0)
    col = lax.broadcasted_iota(jnp.int32, (64, 512), 1)
    owner = 2 * (2 * member + ((r >> 3) & 1)) + ((r >> 4) & 1)
    pick = (col == 32 * owner + 8 * (2 * (r >> 5) + pair) + (r & 7)).astype(bf16)
    both = lax.dot_general(pick, basis_v[...], NT, preferred_element_type=f32).astype(bf16)
    picked[0, 0, 0] = both[:32]
    picked[1, 0, 0] = both[32:]

    with scope("greet"):
        pl.semaphore_wait(barrier, len(greeted))

    def send_columns(t):
        with scope("send_columns%d" % t):
            for d, q in peers:
                pltpu.make_async_remote_copy(
                    picked.at[t, 0, 0], picked.at[t, 0, d], sent, a1_recv.at[8 if t else d],
                    (2 * q + core, j), MESH,
                ).start()
            pltpu.make_async_remote_copy(
                picked.at[t, 0, 0], picked.at[t, 1, 0], sent, fw_recv.at[8 * t], sibling, MESH
            ).start()

    send_columns(0)
    for b in range(16):
        pltpu.make_async_copy(act.at[:, pl.ds(b * depth, depth)], act_v.at[pl.ds(b * depth, depth)], in_sem.at[4]).start()
    for load in loads[1:]:
        load.start()
    pltpu.make_async_remote_copy(
        grads, grads_v.at[core], sent, og_recv, sibling, MESH
    ).start()

    with scope("reorder_basis"):
        row = lax.broadcasted_iota(jnp.int32, (512, 512), 0)
        s = lax.broadcasted_iota(jnp.int32, (512, 512), 1)
        k, pr, d, r = s >> 7, (s >> 6) & 1, (s >> 3) & 7, s & 7
        from_y = (y + 4 - (d & 3)) & 3
        from_x = (x + 2 - (d >> 2)) & 1
        from_core = (core + pr) & 1
        block = 2 * (k >> 1) + ((pair + k) & 1)
        col = 32 * (2 * (2 * from_y + from_x) + from_core) + 8 * block + r
        mix = (row == col).astype(bf16)
        mixed[...] = jnp.dot(basis_v[...], mix, preferred_element_type=f32).astype(bf16)

    with scope("act_wait"):
        pltpu.make_async_copy(act_v, act_v, in_sem.at[4]).wait()

    def partial(k):
        with scope("wait_projected%d" % k):
            drain(table.at[k] if k % 2 else table.at[k, pl.ds(0, 3)], a2_recv.at[k])
        with scope("partial%d" % k):
            left = table[k, :, 0].reshape(64, depth)
            right = table[k, :, 1].reshape(64, depth)
            halves = []
            for h in range(2):
                cols = pl.ds(h * half, half)
                halves.append(
                    jnp.dot(left, grads_v[0, :, cols], preferred_element_type=f32)
                    + jnp.dot(right, grads_v[1, :, cols], preferred_element_type=f32)
                )
            for q in range(8):
                both = [v[8 * q : 8 * q + 8] for v in halves]
                part[k, q] = jnp.concatenate(both, axis=0).astype(bf16)
            for d, q in peers:
                pltpu.make_async_remote_copy(
                    part.at[k, q], got.at[k, d - 1], sent, b_recv.at[k],
                    (2 * q + core, j), MESH,
                ).start()

    def times(t, pr, dy, dx):
        from_chip = ((y + 4 - dy) % 4) * 2 + (x + 2 - dx) % 2
        block = 2 * from_chip + (core + pr) % 2
        rows = act_v[pl.ds(pl.multiple_of(block * depth, depth), depth)]
        return lax.dot_general(picked[t, pr, 4 * dx + dy], rows, NT, preferred_element_type=f32)

    def arrive(n):
        d = NEAR[n][0] + 4 * NEAR[n][1]
        with scope("columns0_%d" % n):
            drain(picked.at[0, 0, d], a1_recv.at[d])
        pltpu.make_async_remote_copy(
            picked.at[0, 0, d], picked.at[0, 1, d], sent, fw_recv.at[d], sibling, MESH
        ).start()

    def sibling_arrive(n):
        d = ALL[n][0] + 4 * ALL[n][1]
        with scope("sibling_columns0"):
            drain(picked.at[0, 1, d], fw_recv.at[d])

    def to_mates(t, acc):
        with scope("to_mates%d" % t):
            k = 2 * t
            acc = acc.astype(bf16)
            proj[t, 0] = acc[:16]
            proj[t, 1] = acc[16:]
            pltpu.make_async_remote_copy(
                proj.at[t, 1 - core], table.at[k, member, core], sent, sib_recv.at[t],
                sibling, MESH,
            ).start()
            for mate in mates:
                for to_core, to_dp in ((core, i), (1 - core, twin)):
                    pltpu.make_async_remote_copy(
                        proj.at[t, to_core], table.at[k, member, core], sent, a2_recv.at[k],
                        (to_dp, mate), MESH,
                    ).start()
            table[k, member, core] = proj[t, core]

    def to_others(t):
        with scope("to_others%d" % t):
            k = 2 * t
            drain(table.at[k, member, 1 - core], sib_recv.at[t])
            for dz in (next_z, across):
                for to_lo in (0, 1):
                    pltpu.make_async_remote_copy(
                        table.at[k, member], table.at[k + 1, member], sent,
                        a2_recv.at[k + 1], (i, at(dz, to_lo)), MESH,
                    ).start()

    acc = times(0, 0, 0, 0)
    for n, offset in enumerate(NEAR):
        arrive(n)
        if n == 0:
            send_columns(1)
        acc += times(0, 0, *offset)
        if n:
            sibling_arrive(n - 1)
            acc += times(0, 1, *ALL[n - 1])
    for n in (6, 7):
        sibling_arrive(n)
        acc += times(0, 1, *ALL[n])
    to_mates(0, acc)

    rest = pl.ds(1, 7)
    with scope("columns1"):
        drain(picked.at[1, 0, rest], a1_recv.at[8])
    pltpu.make_async_remote_copy(
        picked.at[1, 0, rest], picked.at[1, 1, rest], sent, fw_recv.at[8], sibling, MESH
    ).start()
    acc = times(1, 0, 0, 0)
    for offset in NEAR:
        acc += times(1, 0, *offset)
    total[...] = acc
    to_others(0)
    with scope("sibling_columns1"):
        drain(picked.at[1, 1], fw_recv.at[8])
    acc = total[...]
    for offset in ALL:
        acc += times(1, 1, *offset)
    to_mates(1, acc)

    for load in loads[1:]:
        load.wait()
    drain(grads_v.at[1 - core], og_recv)
    partial(0)
    to_others(1)

    def reduce(k):
        with scope("wait_sums%d" % k):
            drain(got.at[k], b_recv.at[k])
        with scope("adam%d" % k):
            low = part[k, chip].astype(f32)
            for d in range(7):
                low += got[k, d].astype(f32)
            mine = pl.ds(pl.multiple_of(8 * (2 * (k // 2) + (pair + k) % 2), 8), 8)
            rows = []
            for h in range(2):
                cols = pl.ds(h * half, half)
                g = low[8 * h : 8 * h + 8]
                nf = beta_one * first_v[mine, cols] + (1.0 - beta_one) * g
                ns = beta_two * second_v[mine, cols] + (1.0 - beta_two) * g * g
                new_first[mine, cols] = nf
                new_second[mine, cols] = ns
                rows.append(nf / first_fix / (jnp.sqrt(ns / second_fix) + adam_eps))
            held[k, 0, 0] = jnp.concatenate(rows, axis=0).astype(bf16)
            for d, q in peers:
                if d < 5 or RELAY[k] is None:
                    pltpu.make_async_remote_copy(
                        held.at[k, 0, 0], held.at[k, 0, d], sent, c_recv.at[k, slot_sem(d)],
                        (2 * q + core, j), MESH,
                    ).start()
            pltpu.make_async_remote_copy(
                held.at[k, 0, 0], held.at[k, 1, 0], sent, cf_recv.at[k // 2], sibling, MESH
            ).start()

    def pass_on(k, which):
        slots = pl.ds(*((1, 3), (4, 1), (5, 3))[which])
        with scope("rows%d_%d" % (k, which)):
            drain(held.at[k, 0, slots], c_recv.at[k, which])
        pltpu.make_async_remote_copy(
            held.at[k, 0, slots], held.at[k, 1, slots], sent, cf_recv.at[k // 2], sibling, MESH
        ).start()

    def relay(k):
        if RELAY[k] == "y then x":
            pass_on(k, 0)
            pltpu.make_async_remote_copy(
                held.at[k, 0, pl.ds(1, 3)], held.at[k, 0, pl.ds(5, 3)], sent,
                c_recv.at[k, 2], (2 * by_slot[4] + core, j), MESH,
            ).start()
        if RELAY[k] == "x then y":
            pass_on(k, 1)
            for d in (1, 3, 2):
                pltpu.make_async_remote_copy(
                    held.at[k, 0, 4], held.at[k, 0, 4 + d], sent,
                    c_recv.at[k, 2], (2 * by_slot[d] + core, j), MESH,
                ).start()

    def in_order(k, h):
        rows = held[k].reshape(16, 16, half).astype(f32)[:, 8 * h : 8 * h + 8]
        return rows.reshape(128, half).astype(bf16)

    for k in range(1, 4):
        partial(k)
    reduce(0)
    reduce(1)
    reduce(2)
    relay(0)
    reduce(3)
    relay(1)
    relay(2)
    pass_on(0, 1)
    pass_on(0, 2)
    pass_on(1, 0)
    pass_on(1, 2)

    with scope("sibling_rows0"):
        drain(held.at[pl.ds(0, 2), 1], cf_recv.at[0])
    with scope("early_update"):
        for h in range(2):
            for k in range(2):
                rows_v[128 * k : 128 * k + 128, pl.ds(h * half, half)] = in_order(k, h)
        for t in range(2 * half // 256):
            cols = pl.ds(256 * t, 256)
            early[:, cols] = jnp.dot(
                mixed[:, pl.ds(0, 256)], rows_v[:, cols], preferred_element_type=f32
            )
    pass_on(3, 0)
    pass_on(3, 1)
    pass_on(2, 1)
    pass_on(2, 2)
    pass_on(3, 2)

    with scope("wait_sibling_rows"):
        drain(held.at[pl.ds(2, 2), 1], cf_recv.at[1])
    columns, rows = 32 * depth, 16 * half
    count = 2 * 15 * columns + depth * 2 * half + 14 * columns // 2 + 8 * columns + 4 * 22 * rows
    with scope("wait_sent"):
        drain(act_v.at[pl.ds(0, count // depth)], sent)


def finish(held, mixed, early, first_i, second_i, update, first_o, second_o, rows_v, update_v, sem):
    outs = [
        pltpu.make_async_copy(first_i, first_o, sem.at[0]),
        pltpu.make_async_copy(second_i, second_o, sem.at[1]),
    ]
    for out in outs:
        out.start()
    width = update.shape[1]
    half = width // 2
    done = 0
    for h in range(2):
        for k in range(2):
            rows = held[2 + k].reshape(16, 16, half).astype(f32)[:, 8 * h : 8 * h + 8]
            rows_v[128 * k : 128 * k + 128, pl.ds(h * half, half)] = rows.reshape(128, half).astype(bf16)
        while done < width and done + 256 <= (h + 1) * half:
            cols = pl.ds(done, 256)
            late = jnp.dot(mixed[:, pl.ds(256, 256)], rows_v[:, cols], preferred_element_type=f32)
            update_v[:, cols] = (early[:, cols] + late).astype(bf16)
            out = pltpu.make_async_copy(update_v.at[:, cols], update.at[:, cols], sem.at[2 + done // 256])
            out.start()
            outs.append(out)
            done += 256
    with scope("results_out"):
        for out in outs:
            out.wait()


def on_device(act, basis, grads, first, second):
    tokens, depth = act.shape[0], basis.shape[0]
    rank, width = basis.shape[1], grads.shape[1]
    rows = first.shape[0]
    half = width // 2
    dma = pltpu.SemaphoreType.DMA
    anywhere = pl.BlockSpec(memory_space=pl.ANY)
    in_vmem = pl.BlockSpec(memory_space=pltpu.VMEM)
    operands = [pltpu.with_memory_space_constraint(v, pltpu.HBM) for v in (act, basis, grads, first, second)]
    held, mixed, early, new_first, new_second = pl.pallas_call(
        exchange,
        out_shape=(
            pltpu.VMEM((4, 2, 8, 16, half), bf16),
            pltpu.VMEM((depth, rank), bf16),
            pltpu.VMEM((depth, width), f32),
            pltpu.VMEM((rows, width), f32),
            pltpu.VMEM((rows, width), f32),
        ),
        in_specs=[anywhere] * 5,
        out_specs=[in_vmem] * 5,
        scratch_shapes=[
            pltpu.VMEM((16 * tokens, depth), bf16),
            pltpu.VMEM((depth, rank), bf16),
            pltpu.VMEM((2, tokens, width), bf16),
            pltpu.VMEM((rows, width), f32),
            pltpu.VMEM((rows, width), f32),
            pltpu.VMEM((2, 2, 8, 32, depth), bf16),
            pltpu.VMEM((2, 2, 16, tokens), bf16),
            pltpu.VMEM((4, 4, 2, 16, tokens), bf16),
            pltpu.VMEM((4, 8, 16, half), bf16),
            pltpu.VMEM((4, 7, 16, half), bf16),
            pltpu.VMEM((32, tokens), f32),
            pltpu.VMEM((rank // 2, width), bf16),
            dma((5,)), dma, dma, dma((9,)), dma((9,)), dma((2,)), dma((4,)), dma((4,)),
            dma((4, 3)), dma((2,)),
        ],
        compiler_params=pltpu.CompilerParams(
            collective_id=0, has_side_effects=True, vmem_limit_bytes=32 << 20
        ),
    )(*operands)
    return pl.pallas_call(
        finish,
        out_shape=(
            pltpu.HBM((depth, width), bf16),
            pltpu.HBM((rows, width), f32),
            pltpu.HBM((rows, width), f32),
        ),
        in_specs=[in_vmem, in_vmem, in_vmem, anywhere, anywhere],
        out_specs=[anywhere] * 3,
        scratch_shapes=[
            pltpu.VMEM((rank // 2, width), bf16),
            pltpu.VMEM((depth, width), bf16),
            dma((2 + width // 256,)),
        ],
        compiler_params=pltpu.CompilerParams(vmem_limit_bytes=24 << 20),
    )(held, mixed, early, new_first, new_second)


def solution(mesh):
    placed = (P("dp", None), P("dp", None), P("dp", "tensor"), P("dp", "tensor"), P("dp", "tensor"))
    return jax.shard_map(
        on_device,
        mesh=mesh,
        in_specs=placed,
        out_specs=(P("dp", "tensor"), P("dp", "tensor"), P("dp", "tensor")),
        check_vma=False,
    )
```

```python
import jax
import jax.numpy as jnp
from jax import lax
from jax.experimental import pallas as pl
from jax.experimental.pallas import tpu as pltpu
from jax.sharding import PartitionSpec as P

beta_one = 0.9
beta_two = 0.999
first_fix = 1.0 - 0.9**50
second_fix = 1.0 - 0.999**50
adam_eps = 1e-08

MESH = pl.DeviceIdType.MESH
bf16 = jnp.bfloat16
f32 = jnp.float32
scope = jax.named_scope

NEAR = ((1, 0), (3, 0), (0, 1), (2, 0), (1, 1), (3, 1), (2, 1))
ALL = ((0, 0),) + NEAR
RELAY = ("y then x", "x then y", "y then x", None)
NT = (((1,), (1,)), ((), ()))


def drain(ref, sem):
    pltpu.make_async_copy(ref, ref, sem).wait()


def slot_sem(d):
    return 0 if d < 4 else 1 if d == 4 else 2


def exchange(
    act, basis, grads, first, second,
    held, mixed, early, new_first, new_second,
    act_v, basis_v, grads_v, first_v, second_v,
    picked, proj, table, part, got, total, rows_v,
    in_sem, sent, og_recv, a1_recv, fw_recv, sib_recv, a2_recv, b_recv, c_recv, cf_recv,
):
    i, j = lax.axis_index("dp"), lax.axis_index("tensor")
    core, chip = i % 2, i // 2
    y, x = chip // 2, chip % 2
    z, lo = j // 2, j % 2
    pair, odd = (z // 2) % 2, z % 2
    member = 2 * odd + lo
    depth = basis.shape[0]
    half = grads.shape[1] // 2
    twin = 2 * chip + (1 - core)

    sibling = (twin, j)
    peers = [(4 * dx + dy, ((y + dy) % 4) * 2 + (x + dx) % 2) for dy, dx in NEAR]
    by_slot = dict(peers)

    loads = [
        pltpu.make_async_copy(basis, basis_v, in_sem.at[0]),
        pltpu.make_async_copy(grads, grads_v.at[core], in_sem.at[1]),
        pltpu.make_async_copy(first, first_v, in_sem.at[2]),
        pltpu.make_async_copy(second, second_v, in_sem.at[3]),
    ]
    loads[0].start()

    barrier = pltpu.get_barrier_semaphore()
    def at(dz, to_lo):
        return 2 * ((z + 8 + dz) % 8) + to_lo

    mates = [at(0, 1 - lo), at(1 - 2 * odd, 0), at(1 - 2 * odd, 1)]
    next_z, across = 2 * odd - 1, 4 * lo - 2
    greeted = [sibling] + [(2 * q + core, j) for _, q in peers]
    greeted += [(to_dp, mate) for mate in mates for to_dp in (i, twin)]
    greeted += [(i, at(next_z, 0)), (i, at(next_z, 1)), (i, at(2, 0)), (i, at(-2, 1))]
    for device in greeted:
        pl.semaphore_signal(barrier, inc=1, device_id=device, device_id_type=MESH)

    loads[0].wait()
    r = lax.broadcasted_iota(jnp.int32, (64, 512), 0)
    col = lax.broadcasted_iota(jnp.int32, (64, 512), 1)
    owner = 2 * (2 * member + ((r >> 3) & 1)) + ((r >> 4) & 1)
    pick = (col == 32 * owner + 8 * (2 * (r >> 5) + pair) + (r & 7)).astype(bf16)
    both = lax.dot_general(pick, basis_v[...], NT, preferred_element_type=f32).astype(bf16)
    picked[0, 0, 0] = both[:32]
    picked[1, 0, 0] = both[32:]

    with scope("greet"):
        pl.semaphore_wait(barrier, len(greeted))

    def send_columns(t):
        with scope("send_columns%d" % t):
            for d, q in peers:
                pltpu.make_async_remote_copy(
                    picked.at[t, 0, 0], picked.at[t, 0, d], sent, a1_recv.at[8 if t else d],
                    (2 * q + core, j), MESH,
                ).start()
            pltpu.make_async_remote_copy(
                picked.at[t, 0, 0], picked.at[t, 1, 0], sent, fw_recv.at[8 * t], sibling, MESH
            ).start()

    send_columns(0)
    for b in range(16):
        pltpu.make_async_copy(act.at[:, pl.ds(b * depth, depth)], act_v.at[pl.ds(b * depth, depth)], in_sem.at[4]).start()
    for load in loads[1:]:
        load.start()
    pltpu.make_async_remote_copy(
        grads, grads_v.at[core], sent, og_recv, sibling, MESH
    ).start()

    with scope("reorder_basis"):
        row = lax.broadcasted_iota(jnp.int32, (512, 512), 0)
        s = lax.broadcasted_iota(jnp.int32, (512, 512), 1)
        k, pr, d, r = s >> 7, (s >> 6) & 1, (s >> 3) & 7, s & 7
        from_y = (y + 4 - (d & 3)) & 3
        from_x = (x + 2 - (d >> 2)) & 1
        from_core = (core + pr) & 1
        block = 2 * (k >> 1) + ((pair + k) & 1)
        col = 32 * (2 * (2 * from_y + from_x) + from_core) + 8 * block + r
        mix = (row == col).astype(bf16)
        mixed[...] = jnp.dot(basis_v[...], mix, preferred_element_type=f32).astype(bf16)

    with scope("act_wait"):
        pltpu.make_async_copy(act_v, act_v, in_sem.at[4]).wait()

    def partial(k):
        with scope("wait_projected%d" % k):
            drain(table.at[k] if k % 2 else table.at[k, pl.ds(0, 3)], a2_recv.at[k])
        with scope("partial%d" % k):
            left = table[k, :, 0].reshape(64, depth)
            right = table[k, :, 1].reshape(64, depth)
            for start, size in ((0, 512), (512, half - 512)) if k == 0 else ((0, half),):
                halves = []
                for h in range(2):
                    cols = pl.ds(h * half + start, size)
                    halves.append(
                        jnp.dot(left, grads_v[0, :, cols], preferred_element_type=f32)
                        + jnp.dot(right, grads_v[1, :, cols], preferred_element_type=f32)
                    )
                piece = pl.ds(start, size)
                for q in range(8):
                    both = [v[8 * q : 8 * q + 8] for v in halves]
                    part[k, q, :, piece] = jnp.concatenate(both, axis=0).astype(bf16)
                for d, q in peers:
                    pltpu.make_async_remote_copy(
                        part.at[k, q, :, piece], got.at[k, d - 1, :, piece], sent, b_recv.at[k],
                        (2 * q + core, j), MESH,
                    ).start()

    def times(t, pr, dy, dx):
        from_chip = ((y + 4 - dy) % 4) * 2 + (x + 2 - dx) % 2
        block = 2 * from_chip + (core + pr) % 2
        rows = act_v[pl.ds(pl.multiple_of(block * depth, depth), depth)]
        return lax.dot_general(picked[t, pr, 4 * dx + dy], rows, NT, preferred_element_type=f32)

    def arrive(n):
        d = NEAR[n][0] + 4 * NEAR[n][1]
        with scope("columns0_%d" % n):
            drain(picked.at[0, 0, d], a1_recv.at[d])
        pltpu.make_async_remote_copy(
            picked.at[0, 0, d], picked.at[0, 1, d], sent, fw_recv.at[d], sibling, MESH
        ).start()

    def sibling_arrive(n):
        d = ALL[n][0] + 4 * ALL[n][1]
        with scope("sibling_columns0"):
            drain(picked.at[0, 1, d], fw_recv.at[d])

    def to_mates(t, acc):
        with scope("to_mates%d" % t):
            k = 2 * t
            acc = acc.astype(bf16)
            proj[t, 0] = acc[:16]
            proj[t, 1] = acc[16:]
            pltpu.make_async_remote_copy(
                proj.at[t, 1 - core], table.at[k, member, core], sent, sib_recv.at[t],
                sibling, MESH,
            ).start()
            for mate in mates:
                for to_core, to_dp in ((core, i), (1 - core, twin)):
                    pltpu.make_async_remote_copy(
                        proj.at[t, to_core], table.at[k, member, core], sent, a2_recv.at[k],
                        (to_dp, mate), MESH,
                    ).start()
            table[k, member, core] = proj[t, core]

    def to_others(t):
        with scope("to_others%d" % t):
            k = 2 * t
            drain(table.at[k, member, 1 - core], sib_recv.at[t])
            for dz in (next_z, across):
                for to_lo in (0, 1):
                    pltpu.make_async_remote_copy(
                        table.at[k, member], table.at[k + 1, member], sent,
                        a2_recv.at[k + 1], (i, at(dz, to_lo)), MESH,
                    ).start()

    acc = times(0, 0, 0, 0)
    for n, offset in enumerate(NEAR):
        arrive(n)
        if n == 0:
            send_columns(1)
        acc += times(0, 0, *offset)
        if n:
            sibling_arrive(n - 1)
            acc += times(0, 1, *ALL[n - 1])
    for n in (6, 7):
        sibling_arrive(n)
        acc += times(0, 1, *ALL[n])
    to_mates(0, acc)

    rest = pl.ds(1, 7)
    with scope("columns1"):
        drain(picked.at[1, 0, rest], a1_recv.at[8])
    pltpu.make_async_remote_copy(
        picked.at[1, 0, rest], picked.at[1, 1, rest], sent, fw_recv.at[8], sibling, MESH
    ).start()
    acc = times(1, 0, 0, 0)
    for offset in NEAR:
        acc += times(1, 0, *offset)
    total[...] = acc
    to_others(0)
    with scope("sibling_columns1"):
        drain(picked.at[1, 1], fw_recv.at[8])
    acc = total[...]
    for offset in ALL:
        acc += times(1, 1, *offset)
    to_mates(1, acc)

    for load in loads[1:]:
        load.wait()
    drain(grads_v.at[1 - core], og_recv)
    partial(0)
    to_others(1)

    def reduce(k):
        with scope("wait_sums%d" % k):
            drain(got.at[k], b_recv.at[k])
        with scope("adam%d" % k):
            low = part[k, chip].astype(f32)
            for d in range(7):
                low += got[k, d].astype(f32)
            mine = pl.ds(pl.multiple_of(8 * (2 * (k // 2) + (pair + k) % 2), 8), 8)
            rows = []
            for h in range(2):
                cols = pl.ds(h * half, half)
                g = low[8 * h : 8 * h + 8]
                nf = beta_one * first_v[mine, cols] + (1.0 - beta_one) * g
                ns = beta_two * second_v[mine, cols] + (1.0 - beta_two) * g * g
                new_first[mine, cols] = nf
                new_second[mine, cols] = ns
                rows.append(nf / first_fix / (jnp.sqrt(ns / second_fix) + adam_eps))
            held[k, 0, 0] = jnp.concatenate(rows, axis=0).astype(bf16)
            for d, q in peers:
                if d < 5 or RELAY[k] is None:
                    pltpu.make_async_remote_copy(
                        held.at[k, 0, 0], held.at[k, 0, d], sent, c_recv.at[k, slot_sem(d)],
                        (2 * q + core, j), MESH,
                    ).start()
            pltpu.make_async_remote_copy(
                held.at[k, 0, 0], held.at[k, 1, 0], sent, cf_recv.at[k // 2], sibling, MESH
            ).start()

    def pass_on(k, which):
        slots = pl.ds(*((1, 3), (4, 1), (5, 3))[which])
        with scope("rows%d_%d" % (k, which)):
            drain(held.at[k, 0, slots], c_recv.at[k, which])
        pltpu.make_async_remote_copy(
            held.at[k, 0, slots], held.at[k, 1, slots], sent, cf_recv.at[k // 2], sibling, MESH
        ).start()

    def relay(k):
        if RELAY[k] == "y then x":
            pass_on(k, 0)
            pltpu.make_async_remote_copy(
                held.at[k, 0, pl.ds(1, 3)], held.at[k, 0, pl.ds(5, 3)], sent,
                c_recv.at[k, 2], (2 * by_slot[4] + core, j), MESH,
            ).start()
        if RELAY[k] == "x then y":
            pass_on(k, 1)
            for d in (1, 3, 2):
                pltpu.make_async_remote_copy(
                    held.at[k, 0, 4], held.at[k, 0, 4 + d], sent,
                    c_recv.at[k, 2], (2 * by_slot[d] + core, j), MESH,
                ).start()

    def in_order(k, h):
        rows = held[k].reshape(16, 16, half).astype(f32)[:, 8 * h : 8 * h + 8]
        return rows.reshape(128, half).astype(bf16)

    for k in range(1, 4):
        partial(k)
    reduce(0)
    reduce(1)
    reduce(2)
    relay(0)
    reduce(3)
    relay(1)
    relay(2)
    pass_on(0, 1)
    pass_on(0, 2)
    pass_on(1, 0)
    pass_on(1, 2)

    pass_on(2, 1)
    pass_on(3, 0)

    with scope("sibling_rows0"):
        drain(held.at[pl.ds(0, 2), 1], cf_recv.at[0])
    with scope("early_update"):
        for h in range(2):
            for k in range(2):
                rows_v[128 * k : 128 * k + 128, pl.ds(h * half, half)] = in_order(k, h)
        for t in range(2 * half // 256):
            cols = pl.ds(256 * t, 256)
            early[:, cols] = jnp.dot(
                mixed[:, pl.ds(0, 256)], rows_v[:, cols], preferred_element_type=f32
            )
    pass_on(3, 1)
    pass_on(2, 2)
    pass_on(3, 2)

    with scope("wait_sibling_rows"):
        drain(held.at[pl.ds(2, 2), 1], cf_recv.at[1])
    columns, rows = 32 * depth, 16 * half
    count = 2 * 15 * columns + depth * 2 * half + 14 * columns // 2 + 8 * columns + 4 * 22 * rows
    with scope("wait_sent"):
        drain(act_v.at[pl.ds(0, count // depth)], sent)


def finish(held, mixed, early, first_i, second_i, update, first_o, second_o, rows_v, update_v, sem):
    outs = [
        pltpu.make_async_copy(first_i, first_o, sem.at[0]),
        pltpu.make_async_copy(second_i, second_o, sem.at[1]),
    ]
    for out in outs:
        out.start()
    width = update.shape[1]
    half = width // 2
    done = 0
    for h in range(2):
        for k in range(2):
            rows = held[2 + k].reshape(16, 16, half).astype(f32)[:, 8 * h : 8 * h + 8]
            rows_v[128 * k : 128 * k + 128, pl.ds(h * half, half)] = rows.reshape(128, half).astype(bf16)
        while done < width and done + 256 <= (h + 1) * half:
            cols = pl.ds(done, 256)
            late = jnp.dot(mixed[:, pl.ds(256, 256)], rows_v[:, cols], preferred_element_type=f32)
            update_v[:, cols] = (early[:, cols] + late).astype(bf16)
            out = pltpu.make_async_copy(update_v.at[:, cols], update.at[:, cols], sem.at[2 + done // 256])
            out.start()
            outs.append(out)
            done += 256
    with scope("results_out"):
        for out in outs:
            out.wait()


def on_device(act, basis, grads, first, second):
    tokens, depth = act.shape[0], basis.shape[0]
    rank, width = basis.shape[1], grads.shape[1]
    rows = first.shape[0]
    half = width // 2
    dma = pltpu.SemaphoreType.DMA
    anywhere = pl.BlockSpec(memory_space=pl.ANY)
    in_vmem = pl.BlockSpec(memory_space=pltpu.VMEM)
    operands = [pltpu.with_memory_space_constraint(v, pltpu.HBM) for v in (act, basis, grads, first, second)]
    held, mixed, early, new_first, new_second = pl.pallas_call(
        exchange,
        out_shape=(
            pltpu.VMEM((4, 2, 8, 16, half), bf16),
            pltpu.VMEM((depth, rank), bf16),
            pltpu.VMEM((depth, width), f32),
            pltpu.VMEM((rows, width), f32),
            pltpu.VMEM((rows, width), f32),
        ),
        in_specs=[anywhere] * 5,
        out_specs=[in_vmem] * 5,
        scratch_shapes=[
            pltpu.VMEM((16 * tokens, depth), bf16),
            pltpu.VMEM((depth, rank), bf16),
            pltpu.VMEM((2, tokens, width), bf16),
            pltpu.VMEM((rows, width), f32),
            pltpu.VMEM((rows, width), f32),
            pltpu.VMEM((2, 2, 8, 32, depth), bf16),
            pltpu.VMEM((2, 2, 16, tokens), bf16),
            pltpu.VMEM((4, 4, 2, 16, tokens), bf16),
            pltpu.VMEM((4, 8, 16, half), bf16),
            pltpu.VMEM((4, 7, 16, half), bf16),
            pltpu.VMEM((32, tokens), f32),
            pltpu.VMEM((rank // 2, width), bf16),
            dma((5,)), dma, dma, dma((9,)), dma((9,)), dma((2,)), dma((4,)), dma((4,)),
            dma((4, 3)), dma((2,)),
        ],
        compiler_params=pltpu.CompilerParams(
            collective_id=0, has_side_effects=True, vmem_limit_bytes=32 << 20
        ),
    )(*operands)
    return pl.pallas_call(
        finish,
        out_shape=(
            pltpu.HBM((depth, width), bf16),
            pltpu.HBM((rows, width), f32),
            pltpu.HBM((rows, width), f32),
        ),
        in_specs=[in_vmem, in_vmem, in_vmem, anywhere, anywhere],
        out_specs=[anywhere] * 3,
        scratch_shapes=[
            pltpu.VMEM((rank // 2, width), bf16),
            pltpu.VMEM((depth, width), bf16),
            dma((2 + width // 256,)),
        ],
        compiler_params=pltpu.CompilerParams(vmem_limit_bytes=24 << 20),
    )(held, mixed, early, new_first, new_second)


def solution(mesh):
    placed = (P("dp", None), P("dp", None), P("dp", "tensor"), P("dp", "tensor"), P("dp", "tensor"))
    return jax.shard_map(
        on_device,
        mesh=mesh,
        in_specs=placed,
        out_specs=(P("dp", "tensor"), P("dp", "tensor"), P("dp", "tensor")),
        check_vma=False,
    )
```

```python
import jax
import jax.numpy as jnp
from jax import lax
from jax.experimental import pallas as pl
from jax.experimental.pallas import tpu as pltpu
from jax.sharding import PartitionSpec as P

beta_one = 0.9
beta_two = 0.999
first_fix = 1.0 - 0.9**50
second_fix = 1.0 - 0.999**50
adam_eps = 1e-08

MESH = pl.DeviceIdType.MESH
bf16 = jnp.bfloat16
f32 = jnp.float32
scope = jax.named_scope

NEAR = ((1, 0), (3, 0), (0, 1), (2, 0), (1, 1), (3, 1), (2, 1))
ALL = ((0, 0),) + NEAR
RELAY = ("y then x", "x then y", "y then x", None)
NT = (((1,), (1,)), ((), ()))


def drain(ref, sem):
    pltpu.make_async_copy(ref, ref, sem).wait()


def slot_sem(d):
    return 0 if d < 4 else 1 if d == 4 else 2


def exchange(
    act, basis, grads, first, second,
    held, mixed, early, new_first, new_second,
    act_v, basis_v, grads_v, first_v, second_v,
    picked, proj, table, part, got, total, rows_v,
    in_sem, sent, og_recv, a1_recv, fw_recv, sib_recv, a2_recv, b_recv, c_recv, cf_recv,
):
    i, j = lax.axis_index("dp"), lax.axis_index("tensor")
    core, chip = i % 2, i // 2
    y, x = chip // 2, chip % 2
    z, lo = j // 2, j % 2
    pair, odd = (z // 2) % 2, z % 2
    member = 2 * odd + lo
    depth = basis.shape[0]
    half = grads.shape[1] // 2
    twin = 2 * chip + (1 - core)

    sibling = (twin, j)
    peers = [(4 * dx + dy, ((y + dy) % 4) * 2 + (x + dx) % 2) for dy, dx in NEAR]
    by_slot = dict(peers)

    loads = [
        pltpu.make_async_copy(basis, basis_v, in_sem.at[0]),
        pltpu.make_async_copy(grads, grads_v.at[core], in_sem.at[1]),
        pltpu.make_async_copy(first, first_v, in_sem.at[2]),
        pltpu.make_async_copy(second, second_v, in_sem.at[3]),
    ]
    loads[0].start()

    barrier = pltpu.get_barrier_semaphore()
    def at(dz, to_lo):
        return 2 * ((z + 8 + dz) % 8) + to_lo

    mates = [at(0, 1 - lo), at(1 - 2 * odd, 0), at(1 - 2 * odd, 1)]
    next_z, across = 2 * odd - 1, 4 * lo - 2
    greeted = [sibling] + [(2 * q + core, j) for _, q in peers]
    greeted += [(to_dp, mate) for mate in mates for to_dp in (i, twin)]
    greeted += [(i, at(next_z, 0)), (i, at(next_z, 1)), (i, at(2, 0)), (i, at(-2, 1))]
    for device in greeted:
        pl.semaphore_signal(barrier, inc=1, device_id=device, device_id_type=MESH)

    loads[0].wait()
    r = lax.broadcasted_iota(jnp.int32, (64, 512), 0)
    col = lax.broadcasted_iota(jnp.int32, (64, 512), 1)
    owner = 2 * (2 * member + ((r >> 3) & 1)) + ((r >> 4) & 1)
    pick = (col == 32 * owner + 8 * (2 * (r >> 5) + pair) + (r & 7)).astype(bf16)
    both = lax.dot_general(pick, basis_v[...], NT, preferred_element_type=f32).astype(bf16)
    picked[0, 0, 0] = both[:32]
    picked[1, 0, 0] = both[32:]

    with scope("greet"):
        pl.semaphore_wait(barrier, len(greeted))

    def send_columns(t):
        with scope("send_columns%d" % t):
            for d, q in peers:
                pltpu.make_async_remote_copy(
                    picked.at[t, 0, 0], picked.at[t, 0, d], sent, a1_recv.at[8 if t else d],
                    (2 * q + core, j), MESH,
                ).start()
            pltpu.make_async_remote_copy(
                picked.at[t, 0, 0], picked.at[t, 1, 0], sent, fw_recv.at[8 * t], sibling, MESH
            ).start()

    send_columns(0)
    for b in range(16):
        pltpu.make_async_copy(act.at[:, pl.ds(b * depth, depth)], act_v.at[pl.ds(b * depth, depth)], in_sem.at[4]).start()
    for load in loads[1:]:
        load.start()
    pltpu.make_async_remote_copy(
        grads, grads_v.at[core], sent, og_recv, sibling, MESH
    ).start()

    with scope("reorder_basis"):
        row = lax.broadcasted_iota(jnp.int32, (512, 512), 0)
        s = lax.broadcasted_iota(jnp.int32, (512, 512), 1)
        k, pr, d, r = s >> 7, (s >> 6) & 1, (s >> 3) & 7, s & 7
        from_y = (y + 4 - (d & 3)) & 3
        from_x = (x + 2 - (d >> 2)) & 1
        from_core = (core + pr) & 1
        block = 2 * (k >> 1) + ((pair + k) & 1)
        col = 32 * (2 * (2 * from_y + from_x) + from_core) + 8 * block + r
        mix = (row == col).astype(bf16)
        mixed[...] = jnp.dot(basis_v[...], mix, preferred_element_type=f32).astype(bf16)

    with scope("act_wait"):
        pltpu.make_async_copy(act_v, act_v, in_sem.at[4]).wait()

    def partial(k):
        with scope("wait_projected%d" % k):
            drain(table.at[k] if k % 2 else table.at[k, pl.ds(0, 3)], a2_recv.at[k])
        with scope("partial%d" % k):
            left = table[k, :, 0].reshape(64, depth)
            right = table[k, :, 1].reshape(64, depth)
            for start, size in ((0, 512), (512, half - 512)) if k == 0 else ((0, half),):
                halves = []
                for h in range(2):
                    cols = pl.ds(h * half + start, size)
                    halves.append(
                        jnp.dot(left, grads_v[0, :, cols], preferred_element_type=f32)
                        + jnp.dot(right, grads_v[1, :, cols], preferred_element_type=f32)
                    )
                piece = pl.ds(start, size)
                for q in range(8):
                    both = [v[8 * q : 8 * q + 8] for v in halves]
                    part[k, q, :, piece] = jnp.concatenate(both, axis=0).astype(bf16)
                for d, q in peers:
                    pltpu.make_async_remote_copy(
                        part.at[k, q, :, piece], got.at[k, d - 1, :, piece], sent, b_recv.at[k],
                        (2 * q + core, j), MESH,
                    ).start()

    def times(t, pr, dy, dx):
        from_chip = ((y + 4 - dy) % 4) * 2 + (x + 2 - dx) % 2
        block = 2 * from_chip + (core + pr) % 2
        rows = act_v[pl.ds(pl.multiple_of(block * depth, depth), depth)]
        return lax.dot_general(picked[t, pr, 4 * dx + dy], rows, NT, preferred_element_type=f32)

    def arrive(n):
        d = NEAR[n][0] + 4 * NEAR[n][1]
        with scope("columns0_%d" % n):
            drain(picked.at[0, 0, d], a1_recv.at[d])
        pltpu.make_async_remote_copy(
            picked.at[0, 0, d], picked.at[0, 1, d], sent, fw_recv.at[d], sibling, MESH
        ).start()

    def sibling_arrive(n):
        d = ALL[n][0] + 4 * ALL[n][1]
        with scope("sibling_columns0"):
            drain(picked.at[0, 1, d], fw_recv.at[d])

    def to_mates(t, acc):
        with scope("to_mates%d" % t):
            k = 2 * t
            acc = acc.astype(bf16)
            proj[t, 0] = acc[:16]
            proj[t, 1] = acc[16:]
            pltpu.make_async_remote_copy(
                proj.at[t, 1 - core], table.at[k, member, core], sent, sib_recv.at[t],
                sibling, MESH,
            ).start()
            for mate in mates:
                for to_core, to_dp in ((core, i), (1 - core, twin)):
                    pltpu.make_async_remote_copy(
                        proj.at[t, to_core], table.at[k, member, core], sent, a2_recv.at[k],
                        (to_dp, mate), MESH,
                    ).start()
            table[k, member, core] = proj[t, core]

    def to_others(t):
        with scope("to_others%d" % t):
            k = 2 * t
            drain(table.at[k, member, 1 - core], sib_recv.at[t])
            for dz in (next_z, across):
                for to_lo in (0, 1):
                    pltpu.make_async_remote_copy(
                        table.at[k, member], table.at[k + 1, member], sent,
                        a2_recv.at[k + 1], (i, at(dz, to_lo)), MESH,
                    ).start()

    acc = times(0, 0, 0, 0)
    for n, offset in enumerate(NEAR):
        arrive(n)
        if n == 0:
            send_columns(1)
        acc += times(0, 0, *offset)
        if n:
            sibling_arrive(n - 1)
            acc += times(0, 1, *ALL[n - 1])
    for n in (6, 7):
        sibling_arrive(n)
        acc += times(0, 1, *ALL[n])
    to_mates(0, acc)

    rest = pl.ds(1, 7)
    with scope("columns1"):
        drain(picked.at[1, 0, rest], a1_recv.at[8])
    pltpu.make_async_remote_copy(
        picked.at[1, 0, rest], picked.at[1, 1, rest], sent, fw_recv.at[8], sibling, MESH
    ).start()
    acc = times(1, 0, 0, 0)
    for offset in NEAR:
        acc += times(1, 0, *offset)
    total[...] = acc
    to_others(0)
    with scope("sibling_columns1"):
        drain(picked.at[1, 1], fw_recv.at[8])
    acc = total[...]
    for offset in ALL:
        acc += times(1, 1, *offset)
    to_mates(1, acc)

    for load in loads[1:]:
        load.wait()
    drain(grads_v.at[1 - core], og_recv)
    partial(0)
    to_others(1)

    def reduce(k):
        with scope("wait_sums%d" % k):
            drain(got.at[k], b_recv.at[k])
        with scope("adam%d" % k):
            low = part[k, chip].astype(f32)
            for d in range(7):
                low += got[k, d].astype(f32)
            mine = pl.ds(pl.multiple_of(8 * (2 * (k // 2) + (pair + k) % 2), 8), 8)
            rows = []
            for h in range(2):
                cols = pl.ds(h * half, half)
                g = low[8 * h : 8 * h + 8]
                nf = beta_one * first_v[mine, cols] + (1.0 - beta_one) * g
                ns = beta_two * second_v[mine, cols] + (1.0 - beta_two) * g * g
                new_first[mine, cols] = nf
                new_second[mine, cols] = ns
                rows.append(nf / first_fix / (jnp.sqrt(ns / second_fix) + adam_eps))
            held[k, 0, 0] = jnp.concatenate(rows, axis=0).astype(bf16)
            for d, q in peers:
                if d < 5 or RELAY[k] is None:
                    pltpu.make_async_remote_copy(
                        held.at[k, 0, 0], held.at[k, 0, d], sent, c_recv.at[k, slot_sem(d)],
                        (2 * q + core, j), MESH,
                    ).start()
            pltpu.make_async_remote_copy(
                held.at[k, 0, 0], held.at[k, 1, 0], sent, cf_recv.at[k // 2], sibling, MESH
            ).start()

    def pass_on(k, which):
        slots = pl.ds(*((1, 3), (4, 1), (5, 3))[which])
        with scope("rows%d_%d" % (k, which)):
            drain(held.at[k, 0, slots], c_recv.at[k, which])
        pltpu.make_async_remote_copy(
            held.at[k, 0, slots], held.at[k, 1, slots], sent, cf_recv.at[k // 2], sibling, MESH
        ).start()

    def relay(k):
        if RELAY[k] == "y then x":
            pass_on(k, 0)
            pltpu.make_async_remote_copy(
                held.at[k, 0, pl.ds(1, 3)], held.at[k, 0, pl.ds(5, 3)], sent,
                c_recv.at[k, 2], (2 * by_slot[4] + core, j), MESH,
            ).start()
        if RELAY[k] == "x then y":
            pass_on(k, 1)
            for d in (1, 3, 2):
                pltpu.make_async_remote_copy(
                    held.at[k, 0, 4], held.at[k, 0, 4 + d], sent,
                    c_recv.at[k, 2], (2 * by_slot[d] + core, j), MESH,
                ).start()

    def in_order(k, h):
        rows = held[k].reshape(16, 16, half).astype(f32)[:, 8 * h : 8 * h + 8]
        return rows.reshape(128, half).astype(bf16)

    for k in range(1, 4):
        partial(k)
    reduce(0)
    reduce(1)
    reduce(2)
    relay(0)
    reduce(3)
    relay(1)
    relay(2)
    pass_on(0, 1)
    pass_on(0, 2)
    pass_on(1, 0)
    pass_on(1, 2)

    pass_on(2, 1)
    pass_on(3, 0)

    with scope("sibling_rows0"):
        drain(held.at[pl.ds(0, 2), 1], cf_recv.at[0])
    with scope("early_update"):
        for h in range(2):
            for k in range(2):
                rows_v[128 * k : 128 * k + 128, pl.ds(h * half, half)] = in_order(k, h)
        for t in range(2 * half // 256):
            cols = pl.ds(256 * t, 256)
            early[:, cols] = jnp.dot(
                mixed[:, pl.ds(0, 256)], rows_v[:, cols], preferred_element_type=f32
            )
    pass_on(3, 1)
    pass_on(2, 2)
    pass_on(3, 2)

    with scope("wait_sibling_rows"):
        drain(held.at[pl.ds(2, 2), 1], cf_recv.at[1])
    columns, rows = 32 * depth, 16 * half
    count = 2 * 15 * columns + depth * 2 * half + 14 * columns // 2 + 8 * columns + 4 * 22 * rows
    with scope("wait_sent"):
        drain(act_v.at[pl.ds(0, count // depth)], sent)


def finish(held, mixed, early, first_i, second_i, update, first_o, second_o, rows_v, update_v, sem):
    outs = [
        pltpu.make_async_copy(first_i, first_o, sem.at[0]),
        pltpu.make_async_copy(second_i, second_o, sem.at[1]),
    ]
    for out in outs:
        out.start()
    width = update.shape[1]
    half = width // 2
    for h in range(2):
        for k in range(2):
            rows = held[2 + k].reshape(16, 16, half).astype(f32)[:, 8 * h : 8 * h + 8]
            rows_v[128 * k : 128 * k + 128, pl.ds(h * half, half)] = rows.reshape(128, half).astype(bf16)
    for t in range(update.shape[0] // 128):
        at = pl.ds(128 * t, 128)
        late = jnp.dot(mixed[at, pl.ds(256, 256)], rows_v[...], preferred_element_type=f32)
        update_v[at] = (early[at] + late).astype(bf16)
        out = pltpu.make_async_copy(update_v.at[at], update.at[at], sem.at[2 + t])
        out.start()
        outs.append(out)
    with scope("results_out"):
        for out in outs:
            out.wait()


def on_device(act, basis, grads, first, second):
    tokens, depth = act.shape[0], basis.shape[0]
    rank, width = basis.shape[1], grads.shape[1]
    rows = first.shape[0]
    half = width // 2
    dma = pltpu.SemaphoreType.DMA
    anywhere = pl.BlockSpec(memory_space=pl.ANY)
    in_vmem = pl.BlockSpec(memory_space=pltpu.VMEM)
    operands = [pltpu.with_memory_space_constraint(v, pltpu.HBM) for v in (act, basis, grads, first, second)]
    held, mixed, early, new_first, new_second = pl.pallas_call(
        exchange,
        out_shape=(
            pltpu.VMEM((4, 2, 8, 16, half), bf16),
            pltpu.VMEM((depth, rank), bf16),
            pltpu.VMEM((depth, width), f32),
            pltpu.VMEM((rows, width), f32),
            pltpu.VMEM((rows, width), f32),
        ),
        in_specs=[anywhere] * 5,
        out_specs=[in_vmem] * 5,
        scratch_shapes=[
            pltpu.VMEM((16 * tokens, depth), bf16),
            pltpu.VMEM((depth, rank), bf16),
            pltpu.VMEM((2, tokens, width), bf16),
            pltpu.VMEM((rows, width), f32),
            pltpu.VMEM((rows, width), f32),
            pltpu.VMEM((2, 2, 8, 32, depth), bf16),
            pltpu.VMEM((2, 2, 16, tokens), bf16),
            pltpu.VMEM((4, 4, 2, 16, tokens), bf16),
            pltpu.VMEM((4, 8, 16, half), bf16),
            pltpu.VMEM((4, 7, 16, half), bf16),
            pltpu.VMEM((32, tokens), f32),
            pltpu.VMEM((rank // 2, width), bf16),
            dma((5,)), dma, dma, dma((9,)), dma((9,)), dma((2,)), dma((4,)), dma((4,)),
            dma((4, 3)), dma((2,)),
        ],
        compiler_params=pltpu.CompilerParams(
            collective_id=0, has_side_effects=True, vmem_limit_bytes=32 << 20
        ),
    )(*operands)
    return pl.pallas_call(
        finish,
        out_shape=(
            pltpu.HBM((depth, width), bf16),
            pltpu.HBM((rows, width), f32),
            pltpu.HBM((rows, width), f32),
        ),
        in_specs=[in_vmem, in_vmem, in_vmem, anywhere, anywhere],
        out_specs=[anywhere] * 3,
        scratch_shapes=[
            pltpu.VMEM((rank // 2, width), bf16),
            pltpu.VMEM((depth, width), bf16),
            dma((2 + depth // 128,)),
        ],
        compiler_params=pltpu.CompilerParams(vmem_limit_bytes=24 << 20),
    )(held, mixed, early, new_first, new_second)


def solution(mesh):
    placed = (P("dp", None), P("dp", None), P("dp", "tensor"), P("dp", "tensor"), P("dp", "tensor"))
    return jax.shard_map(
        on_device,
        mesh=mesh,
        in_specs=placed,
        out_specs=(P("dp", "tensor"), P("dp", "tensor"), P("dp", "tensor")),
        check_vma=False,
    )
```
